32 devices in a mesh: seq: 4 (over z), head: 4 (over y, x), req: 2 (over core).
Axes of the slice: x: 2, y: 2, z: 4, core: 2. Of those that a mesh axis runs over, the one named last changes fastest.
Arguments:
- queries: bfloat16 [8, 512, 128], P('req', ('head', 'seq')), may hold values from -256 to 256
- key_codes: bfloat16 [8, 8, 2048, 128], P('req', 'head', 'seq'), may hold values from -448 to 448
- key_scale: float32 [8, 8, 32], P('req', 'head', 'seq'), may hold values from 0.01 to 0.1
- value_codes: bfloat16 [8, 8, 2048, 128], P('req', 'head', 'seq'), may hold values from -192 to 192
- value_scale: float32 [8, 8, 32], P('req', 'head', 'seq'), may hold values from 0.01 to 0.06
- out_weight: bfloat16 [16384, 16384], P('head', 'seq'), may hold values from -0.1875 to 0.1875
- ctx_len: int32 [8], P('req'), may hold values from 512 to 2048, as said below
- start_shard: int32 [8], P('req'), may hold values from 0 to 3
- draft_depth: int32 [8, 4], P('req'), may hold values from 0 to 3
Outputs:
- projected: bfloat16 [4, 8, 16384], P('head', 'req', 'seq')
The draws below stay inside these ranges and needn't reach their ends.
Inputs may be any that keep to these rules, and one draw needn't show every extreme that they name: `ctx_len`: at least one request has exactly 2048 positions.
All inputs are finite; a program needn't handle non-finite values.
Results may differ from the reference program's by a relative error of at most 0.0057.
Values may be sent and summed in bfloat16 or wider, within the bound.
No kernel may reach another device: no remote copies, remote signals or barrier semaphores. Data moves between devices by JAX's collectives and lax.ppermute only.
A program may use at most 64 MiB of HBM per device.

```python
import math
import jax
import jax.numpy as jnp
from jax import lax

D = 16384
QHEADS = 128
KVH = 8
HD = 128
DRAFT = 4
BLK = 64
KV_DEV = 512
REQS = 8
CTX = 2048
N_SEQ = 4


def world(key):
    parts = jax.random.split(key, 8)
    shard_count = CTX // KV_DEV
    lengths = jax.random.randint(parts[0], (REQS,), CTX // 4, CTX + 1)
    longest = jax.random.randint(parts[1], (), 0, REQS)
    lengths = jnp.where(jnp.arange(REQS) == longest, CTX, lengths).astype(jnp.int32)
    starts = jax.random.randint(parts[2], (REQS,), 0, shard_count)
    last_pick = jax.random.randint(parts[6], (), 0, REQS)
    first_pick = jnp.mod(last_pick + 1 + jax.random.randint(parts[7], (), 0, REQS - 1), REQS)
    request_ids = jnp.arange(REQS)
    starts = jnp.where(request_ids == last_pick, shard_count - 1, starts)
    starts = jnp.where(request_ids == first_pick, 0, starts).astype(jnp.int32)
    depths = jax.random.randint(parts[3], (REQS, DRAFT), 0, DRAFT).astype(jnp.int32)
    codes = jnp.clip(32.0 * jax.random.normal(parts[4], (REQS, KVH, CTX, HD), jnp.float32), -448.0, 448.0).astype(jnp.bfloat16)
    scales = jnp.exp(jax.random.uniform(parts[5], (REQS, KVH, CTX // BLK), jnp.float32, math.log(0.01), math.log(0.1)))
    return (lengths, starts, depths, codes, scales)


def draw_ctx_len(key, part):
    return world(key)[0]


def draw_start_shard(key, part):
    return world(key)[1]


def draw_draft_depth(key, part):
    return world(key)[2]


def draw_key_codes(key, part):
    return world(key)[3]


def draw_key_scale(key, part):
    return world(key)[4]


def draw_queries(key, part):
    lengths, starts, depths, codes, scales = world(key)
    extra = jax.random.split(jax.random.fold_in(key, 91), 3)
    group = QHEADS // KVH
    shard_count = CTX // KV_DEV
    own_pos = lengths[:, None] - DRAFT + depths
    tie_pos = jax.random.randint(extra[0], (REQS, DRAFT), 0, 1 << 20) % (lengths[:, None] - DRAFT)

    def fetch(position):
        where_at = jnp.mod(starts[:, None] + position // KV_DEV, shard_count) * KV_DEV + position % KV_DEV
        picked = jnp.take_along_axis(codes, where_at[:, None, :, None], axis=2).astype(jnp.float32)
        factor = jnp.take_along_axis(scales, (where_at // BLK)[:, None, :], axis=2)
        return picked * factor[..., None]
    own = fetch(own_pos)
    tie = fetch(tie_pos)
    root = math.sqrt(HD)
    g_one = (jnp.sum(own * own, axis=-1) / root)[:, :, None, :]
    g_mix = (jnp.sum(own * tie, axis=-1) / root)[:, :, None, :]
    g_two = (jnp.sum(tie * tie, axis=-1) / root)[:, :, None, :]
    strength = jax.random.uniform(extra[1], (REQS, KVH, group, DRAFT), jnp.float32, 3.0, 8.0)
    second = jnp.where(strength > 0.0, strength - 2.0, 0.0)
    determinant = g_one * g_two - g_mix * g_mix
    alpha = (g_two * strength - g_mix * second) / determinant
    beta = (g_one * second - g_mix * strength) / determinant
    unit_one = own / jnp.sqrt(jnp.sum(own * own, axis=-1, keepdims=True))
    remainder = tie - jnp.sum(tie * unit_one, axis=-1, keepdims=True) * unit_one
    unit_two = remainder / jnp.sqrt(jnp.sum(remainder * remainder, axis=-1, keepdims=True))
    unit_one = unit_one[:, :, None]
    unit_two = unit_two[:, :, None]
    noise = jax.random.normal(extra[2], (REQS, KVH, group, DRAFT, HD), jnp.float32)
    noise = noise - jnp.sum(noise * unit_one, axis=-1, keepdims=True) * unit_one
    noise = noise - jnp.sum(noise * unit_two, axis=-1, keepdims=True) * unit_two
    values = noise + alpha[..., None] * own[:, :, None] + beta[..., None] * tie[:, :, None]
    return jnp.clip(values, -256.0, 256.0).reshape(REQS, QHEADS * DRAFT, HD).astype(jnp.bfloat16)


def block_scale(stream_key, extent, cuts, smallest, high):
    loudness, own = 1.0, jax.random.fold_in(stream_key, 6)
    for dim, blocks in cuts:
        heights = jnp.exp(jax.random.uniform(jax.random.fold_in(own, dim), (blocks,), jnp.float32, smallest / len(cuts), high / len(cuts)))
        loudness = loudness * jnp.repeat(heights, extent[dim] // blocks).reshape([-1 if axis == dim else 1 for axis in range(len(extent))])
    return loudness


def scatter_about(key, extent, scale, limit, shards=(), kind=jnp.bfloat16):
    drawn = jax.random.normal(key, extent, jnp.float32) * scale
    if len(shards) > 0:
        drawn = block_scale(key, extent, shards, -0.22, 0.18) * drawn
    return jnp.clip(drawn, min=-limit, max=limit).astype(kind)


def setup_inputs(seed: int = 0) -> dict:
    seeds = jax.random.split(jax.random.key(seed), 10)
    return {
        "queries": draw_queries(jax.random.fold_in(seeds[9], 71), 0),
        "key_codes": draw_key_codes(jax.random.fold_in(seeds[9], 71), 0),
        "key_scale": draw_key_scale(jax.random.fold_in(seeds[9], 71), 0),
        "value_codes": scatter_about(seeds[3], (REQS, KVH, CTX, HD), 32.0, 192.0, ((0, 2), (1, 4), (2, 4))),
        "value_scale": jnp.clip(jnp.exp(math.log(0.06) - 1.7917595 * jax.random.uniform(seeds[4], (REQS, KVH, CTX // BLK), jnp.float32) ** block_scale(seeds[4], (REQS, KVH, CTX // BLK), ((0, 2), (1, 4), (2, 4)), -0.2, 0.2)), 0.01, 0.06),
        "out_weight": scatter_about(seeds[5], (QHEADS * HD, D), (KVH * HD) ** -0.5, 0.1875, ((0, 4), (1, 4))),
        "ctx_len": draw_ctx_len(jax.random.fold_in(seeds[9], 71), 0),
        "start_shard": draw_start_shard(jax.random.fold_in(seeds[9], 71), 0),
        "draft_depth": draw_draft_depth(jax.random.fold_in(seeds[9], 71), 0),
    }


NEG_FLOOR = -1e+30

def combine_state(first, second):
    top = jnp.maximum(first[0], second[0])
    early = jnp.exp(first[0] - top)
    later = jnp.exp(second[0] - top)
    return (top, first[1] * early + second[1] * later, first[2] * early[..., None] + second[2] * later[..., None])

def shard_partial(block_q, key_block, key_tok, value_block, value_tok, positions, limits):
    raw = jnp.einsum('rhqd,rhkd->rhqk', block_q.astype(jnp.float32), key_block.astype(jnp.float32))
    scores = raw * (key_tok[:, :, None, :] * (1.0 / math.sqrt(HD)))
    visible = positions[:, None, None, :] <= limits[:, None, :, None]
    masked = jnp.where(visible, scores, NEG_FLOOR)
    top = lax.optimization_barrier(jnp.max(masked, axis=3))
    weights = jnp.where(visible, jnp.exp(masked - top[..., None]), 0.0)
    total = lax.optimization_barrier(jnp.sum(weights, axis=3))
    scaled = (weights * value_tok[:, :, None, :]).astype(jnp.bfloat16)
    acc = jnp.einsum('rhqk,rhkd->rhqd', scaled.astype(jnp.float32), value_block.astype(jnp.float32))
    return (top, total, acc)

def reference(queries, key_codes, key_scale, value_codes, value_scale, out_weight, ctx_len, start_shard, draft_depth):
    group_rows = QHEADS // KVH * DRAFT
    grouped = queries.reshape(REQS, KVH, group_rows, HD)
    draft_of = jnp.arange(group_rows, dtype=jnp.int32) % DRAFT
    limits = (ctx_len - DRAFT)[:, None] + draft_depth[:, draft_of]
    per_shard = KV_DEV // BLK

    def visit(state, shard):
        key_block = lax.dynamic_slice_in_dim(key_codes, shard * KV_DEV, KV_DEV, 2)
        value_block = lax.dynamic_slice_in_dim(value_codes, shard * KV_DEV, KV_DEV, 2)
        key_tok = jnp.repeat(lax.dynamic_slice_in_dim(key_scale, shard * per_shard, per_shard, 2), BLK, axis=2)
        value_tok = jnp.repeat(lax.dynamic_slice_in_dim(value_scale, shard * per_shard, per_shard, 2), BLK, axis=2)
        positions = jnp.mod(shard - start_shard, N_SEQ)[:, None] * KV_DEV + jnp.arange(KV_DEV, dtype=jnp.int32)[None, :]
        part = shard_partial(grouped, key_block, key_tok, value_block, value_tok, positions, limits)
        return (combine_state(state, part), None)
    start_state = (jnp.full((REQS, KVH, group_rows), NEG_FLOOR, jnp.float32), jnp.zeros((REQS, KVH, group_rows), jnp.float32), jnp.zeros((REQS, KVH, group_rows, HD), jnp.float32))
    final, unused = lax.scan(visit, start_state, jnp.arange(N_SEQ, dtype=jnp.int32))
    attention = (final[2] / final[1][..., None]).astype(jnp.bfloat16)
    arranged = attention.reshape(REQS, QHEADS, DRAFT, HD)
    flat = jnp.transpose(arranged, (2, 0, 1, 3)).reshape(DRAFT * REQS, QHEADS * HD)
    result = jnp.dot(flat, out_weight, preferred_element_type=jnp.float32)
    return result.reshape(DRAFT, REQS, D).astype(jnp.bfloat16)
```

```python
import functools
import math

import jax
import jax.numpy as jnp
from jax import lax
from jax.experimental import pallas as pl
from jax.experimental.pallas import tpu as pltpu
from jax.sharding import PartitionSpec as P

QHEADS = 128
KVH = 8
HD = 128
DRAFT = 4
BLK = 64

NEG_FLOOR = -1e30
STAT_ROWS = 16
MIB = 1 << 20
VMEM = pl.BlockSpec(memory_space=pltpu.VMEM)
SMEM = pl.BlockSpec(memory_space=pltpu.SMEM)


def swapped(value, axis, step):
    count = lax.axis_size(axis)
    return lax.ppermute(value, axis, [(source, source ^ step) for source in range(count)])


def in_vmem(value):
    return pltpu.with_memory_space_constraint(value, pltpu.VMEM)


def kernel_call(kernel, out_shape, in_specs, flops, limit, scratch=()):
    return pl.pallas_call(
        kernel,
        out_shape=out_shape,
        in_specs=in_specs,
        out_specs=jax.tree.map(lambda _: VMEM, out_shape),
        scratch_shapes=list(scratch),
        cost_estimate=pl.CostEstimate(flops=flops, bytes_accessed=0, transcendentals=0),
        compiler_params=pltpu.CompilerParams(vmem_limit_bytes=limit),
    )


def three_parts(value):
    high = value.astype(jnp.bfloat16).astype(jnp.float32)
    rest = value - high
    middle = rest.astype(jnp.bfloat16).astype(jnp.float32)
    return (high, middle, rest - middle)


def attend_kernel(steps, group_rows, *refs):
    count = len(steps)
    ctx, start, depth, key_scale, value_scale = refs[:5]
    q_refs = refs[5 : 5 + count]
    key_ref, value_ref = refs[5 + count : 7 + count]
    out_refs = refs[7 + count :]
    req_dev, rows_dev, head_dim = q_refs[0].shape
    kv_rows = key_ref.shape[2]
    blocks = key_scale.shape[2]
    width = kv_rows // blocks
    drafts = depth.shape[1]
    seq_count = lax.axis_size("seq")
    here = lax.axis_index("seq")
    lane = lax.broadcasted_iota(jnp.int32, (1, kv_rows), 1)
    draft_of = lax.broadcasted_iota(jnp.int32, (rows_dev, 1), 0) % drafts
    stat_lane = lax.broadcasted_iota(jnp.int32, (rows_dev, head_dim), 1)
    inverse = 1.0 / math.sqrt(head_dim)

    def spread(scale_ref, req, head, factor):
        found = jnp.full((1, kv_rows), scale_ref[req, head, 0] * factor, jnp.float32)
        for block in range(1, blocks):
            found = jnp.where(lane >= block * width, scale_ref[req, head, block] * factor, found)
        return found

    for index, step in enumerate(steps):
        head = (here ^ step) * rows_dev // group_rows
        stats = []
        for req in range(req_dev):
            first = jnp.where(here >= start[req], here - start[req], here - start[req] + seq_count)
            position = first * kv_rows + lane
            limit = jnp.full((rows_dev, 1), depth[req, 0], jnp.int32)
            for draft in range(1, drafts):
                limit = jnp.where(draft_of == draft, depth[req, draft], limit)
            limit = limit + (ctx[req] - drafts)
            raw = lax.dot_general(
                q_refs[index][req],
                key_ref[req, head],
                (((1,), (1,)), ((), ())),
                preferred_element_type=jnp.float32,
            )
            visible = position <= limit
            masked = jnp.where(visible, raw * spread(key_scale, req, head, inverse), NEG_FLOOR)
            top = jnp.max(masked, axis=1, keepdims=True)
            weights = jnp.where(visible, jnp.exp(masked - top), 0.0)
            total = jnp.sum(weights, axis=1, keepdims=True)
            scaled = (weights * spread(value_scale, req, head, 1.0)).astype(jnp.bfloat16)
            acc = jnp.dot(scaled, value_ref[req, head], preferred_element_type=jnp.float32)
            out_refs[index][req * rows_dev : (req + 1) * rows_dev, :] = acc.astype(jnp.bfloat16)
            found = jnp.zeros((rows_dev, head_dim), jnp.float32)
            for at, part in enumerate(three_parts(top) + three_parts(total)):
                found = jnp.where(stat_lane == at, part, found)
            stats.append(found)
        turned = jnp.transpose(jnp.concatenate(stats, axis=0))
        out_refs[index][req_dev * rows_dev :, :] = turned[:STAT_ROWS].astype(jnp.bfloat16)


def merge_kernel(req_dev, rows_dev, drafts, *refs):
    part_refs = refs[:-3]
    out_ref, held, ordered = refs[-3:]
    rows = req_dev * rows_dev
    heads = rows_dev // drafts
    head_count = lax.axis_size("head")
    share = drafts // head_count
    mine = lax.axis_index("head")
    stats = [ref[rows:, :].astype(jnp.float32) for ref in part_refs]
    tops = [stat[0:1] + stat[1:2] + stat[2:3] for stat in stats]
    totals = [stat[3:4] + stat[4:5] + stat[5:6] for stat in stats]
    top = functools.reduce(jnp.maximum, tops)
    factors = [jnp.exp(value - top) for value in tops]
    total = sum(value * factor for value, factor in zip(totals, factors))
    lanes = top.shape[1]
    which = lax.broadcasted_iota(jnp.int32, (lanes, lanes), 0)
    table = jnp.zeros((lanes, lanes), jnp.float32)
    for at, factor in enumerate(factors):
        table = jnp.where(which == at, factor / total, table)
    turned = jnp.transpose(table)
    merged = sum(
        ref[:rows, :].astype(jnp.float32) * turned[:, at : at + 1]
        for at, ref in enumerate(part_refs)
    )
    held[...] = merged
    for req in range(req_dev):
        for draft in range(drafts):
            taken = held[pl.ds(req * rows_dev + draft, heads, stride=drafts), :]
            place = (draft // share) ^ mine
            row = (place * share + draft % share) * req_dev + req
            ordered[pl.ds(row, heads, stride=drafts * req_dev), :] = taken
    out_ref[...] = ordered[...].astype(jnp.bfloat16)


def project_kernel(steps, *refs):
    count = len(steps)
    x_refs = refs[:count]
    weight_ref = refs[count]
    out_refs = refs[count + 1 :]
    rows, head_dim = x_refs[0].shape
    here = lax.axis_index("seq")
    pieces = len(out_refs)
    tall = out_refs[0].shape[0]
    depth = weight_ref.shape[0] // lax.axis_size("seq")
    heads = depth // head_dim
    lines = rows // heads
    x_parts = [
        jnp.concatenate(
            [ref[head * lines : (head + 1) * lines, :] for head in range(heads)], axis=1
        )
        for ref in x_refs
    ]
    wide = weight_ref.shape[1]
    cut = min(wide, 512)
    for column in range(0, wide, cut):
        found = jnp.zeros((lines, cut), jnp.float32)
        for step, part in zip(steps, x_parts):
            first = pl.multiple_of((here ^ step) * depth, depth)
            found = found + jnp.dot(
                part,
                weight_ref[pl.ds(first, depth), column : column + cut],
                preferred_element_type=jnp.float32,
            )
        for piece, out_ref in enumerate(out_refs):
            out_ref[:, column : column + cut] = found[piece * tall : (piece + 1) * tall].astype(
                out_ref.dtype
            )


def sum_kernel(*refs):
    out_ref = refs[-1]
    total = refs[0][...].astype(jnp.float32)
    for ref in refs[1:-1]:
        total = total + ref[...].astype(jnp.float32)
    out_ref[...] = total.astype(out_ref.dtype).reshape(out_ref.shape)


def with_kernels(
    queries,
    key_codes,
    key_scale,
    value_codes,
    value_scale,
    out_weight,
    ctx_len,
    start_shard,
    draft_depth,
):
    seq_count = lax.axis_size("seq")
    head_count = lax.axis_size("head")
    req_dev, rows_dev, head_dim = queries.shape
    group_rows = seq_count * rows_dev // key_codes.shape[1]
    drafts = draft_depth.shape[1]
    rows = req_dev * rows_dev
    wide = out_weight.shape[1]
    others = range(1, seq_count)
    payload = jax.ShapeDtypeStruct((rows + STAT_ROWS, head_dim), jnp.bfloat16)

    keys, values = in_vmem(key_codes), in_vmem(value_codes)

    def attend(steps, blocks):
        return kernel_call(
            functools.partial(attend_kernel, steps, group_rows),
            [payload] * len(steps),
            [SMEM] * 5 + [VMEM] * (len(steps) + 2),
            20_000_000_000,
            8 * MIB,
        )(ctx_len, start_shard, draft_depth, key_scale, value_scale, *blocks, keys, values)

    arrived = [swapped(queries, "seq", step) for step in others]
    own = attend((0,), [queries])
    partials = attend(tuple(others), arrived)
    returned = [swapped(part, "seq", step) for step, part in zip(others, partials)]
    finished = kernel_call(
        functools.partial(merge_kernel, req_dev, rows_dev, drafts),
        jax.ShapeDtypeStruct((rows, head_dim), jnp.bfloat16),
        [VMEM] * seq_count,
        20_000_000_000,
        4 * MIB,
        [pltpu.VMEM((rows, head_dim), jnp.float32)] * 2,
    )(*own, *returned)
    gathered = [finished] + [swapped(finished, "seq", step) for step in others]
    tall = drafts // head_count * req_dev
    shares = kernel_call(
        functools.partial(project_kernel, tuple(range(seq_count))),
        [jax.ShapeDtypeStruct((tall, wide), jnp.bfloat16)] * head_count,
        [VMEM] * (seq_count + 1),
        20_000_000_000,
        8 * MIB,
    )(*gathered, in_vmem(out_weight))
    summed = [shares[0]] + [swapped(shares[step], "head", step) for step in range(1, head_count)]
    return kernel_call(
        sum_kernel,
        jax.ShapeDtypeStruct((drafts // head_count, req_dev, wide), jnp.bfloat16),
        [VMEM] * head_count,
        1_000_000,
        4 * MIB,
    )(*summed)


def passed_along(value, axis, steps):
    count = lax.axis_size(axis)
    pairs = [(source, (source + steps) % count) for source in range(count)]
    return lax.ppermute(value, axis, pairs)


def combine_state(first, second):
    top = jnp.maximum(first[0], second[0])
    early = jnp.exp(first[0] - top)
    later = jnp.exp(second[0] - top)
    return (
        top,
        first[1] * early + second[1] * later,
        first[2] * early[..., None] + second[2] * later[..., None],
    )


def shard_partial(block_q, key_block, key_tok, value_block, value_tok, positions, limits):
    raw = jnp.einsum("rhqd,rhkd->rhqk", block_q, key_block, preferred_element_type=jnp.float32)
    scores = raw * (key_tok[:, :, None, :] * (1.0 / math.sqrt(HD)))
    visible = positions[:, None, None, :] <= limits[:, None, :, None]
    masked = jnp.where(visible, scores, NEG_FLOOR)
    top = jnp.max(masked, axis=3)
    weights = jnp.where(visible, jnp.exp(masked - top[..., None]), 0.0)
    total = jnp.sum(weights, axis=3)
    scaled = (weights * value_tok[:, :, None, :]).astype(jnp.bfloat16)
    acc = jnp.einsum("rhqk,rhkd->rhqd", scaled, value_block, preferred_element_type=jnp.float32)
    return (top, total, acc)


def round_the_ring(
    queries,
    key_codes,
    key_scale,
    value_codes,
    value_scale,
    out_weight,
    ctx_len,
    start_shard,
    draft_depth,
):
    seq_count = lax.axis_size("seq")
    here = lax.axis_index("seq")
    req_dev, rows_dev, head_dim = queries.shape
    kv_rows = key_codes.shape[2]
    group_rows = QHEADS // KVH * DRAFT
    key_tok = jnp.repeat(key_scale, BLK, axis=2)
    value_tok = jnp.repeat(value_scale, BLK, axis=2)
    offsets = jnp.mod(here - start_shard, seq_count)
    positions = offsets[:, None] * kv_rows + jnp.arange(kv_rows, dtype=jnp.int32)[None, :]
    base_limit = ctx_len - DRAFT
    draft_ids = jnp.arange(DRAFT, dtype=jnp.int32)

    def row_limits(first, count):
        draft_of = (first + jnp.arange(count, dtype=jnp.int32)) % DRAFT
        pick = (draft_of[:, None] == draft_ids[None, :]).astype(jnp.int32)
        return base_limit[:, None] + jnp.sum(draft_depth[:, None, :] * pick[None], axis=2)

    def turn(step, carry):
        block_q, top, total, acc = carry
        anchor = jnp.mod(here - step, seq_count)
        first = anchor * rows_dev
        head_pick = first // group_rows
        key_block = lax.dynamic_slice_in_dim(key_codes, head_pick, 1, 1)
        value_block = lax.dynamic_slice_in_dim(value_codes, head_pick, 1, 1)
        key_sel = lax.dynamic_slice_in_dim(key_tok, head_pick, 1, 1)
        value_sel = lax.dynamic_slice_in_dim(value_tok, head_pick, 1, 1)
        part = shard_partial(
            block_q[:, None],
            key_block,
            key_sel,
            value_block,
            value_sel,
            positions,
            row_limits(first, rows_dev),
        )
        merged = combine_state((top, total, acc), (part[0][:, 0], part[1][:, 0], part[2][:, 0]))
        moved = passed_along(
            (block_q.astype(jnp.float32), merged[0], merged[1], merged[2]), "seq", 1
        )
        return (moved[0].astype(jnp.bfloat16), moved[1], moved[2], moved[3])

    start_state = (
        queries,
        jnp.full((req_dev, rows_dev), NEG_FLOOR, jnp.float32),
        jnp.zeros((req_dev, rows_dev), jnp.float32),
        jnp.zeros((req_dev, rows_dev, head_dim), jnp.float32),
    )
    final = lax.fori_loop(0, seq_count, turn, start_state)
    attention = (final[3] / final[2][..., None]).astype(jnp.bfloat16)
    gathered = lax.all_gather(attention, "seq", axis=1, tiled=True)
    heads = gathered.shape[1] // DRAFT
    arranged = gathered.reshape(req_dev, heads, DRAFT, head_dim)
    width_dev = out_weight.shape[1]
    flat = jnp.transpose(arranged, (2, 0, 1, 3)).reshape(DRAFT * req_dev, heads * head_dim)
    result = jnp.dot(flat, out_weight, preferred_element_type=jnp.float32)
    summed = lax.psum_scatter(
        result.reshape(DRAFT, req_dev, width_dev), "head", scatter_dimension=0, tiled=True
    )
    return summed.astype(jnp.bfloat16)


def on_device(*arrays):
    queries, key_codes = arrays[:2]
    seq_count, head_count = lax.axis_size("seq"), lax.axis_size("head")
    req_dev, rows_dev, head_dim = queries.shape
    paired = all(count & (count - 1) == 0 for count in (seq_count, head_count))
    tiled = req_dev * rows_dev == head_dim and rows_dev % (2 * DRAFT) == 0
    whole = seq_count * rows_dev // key_codes.shape[1] % rows_dev == 0
    if paired and tiled and whole and DRAFT % head_count == 0:
        return with_kernels(*arrays)
    return round_the_ring(*arrays)


def solution(mesh):
    placed = (
        P("req", ("head", "seq"), None),
        P("req", "head", "seq", None),
        P("req", "head", "seq"),
        P("req", "head", "seq", None),
        P("req", "head", "seq"),
        P("head", "seq"),
        P("req"),
        P("req"),
        P("req", None),
    )
    return jax.shard_map(
        on_device, mesh=mesh, in_specs=placed, out_specs=P("head", "req", "seq"), check_vma=False
    )
```

```python
import functools
import math

import jax
import jax.numpy as jnp
from jax import lax
from jax.experimental import pallas as pl
from jax.experimental.pallas import tpu as pltpu
from jax.sharding import PartitionSpec as P

QHEADS = 128
KVH = 8
HD = 128
DRAFT = 4
BLK = 64

NEG_FLOOR = -1e30
STAT_ROWS = 16
MIB = 1 << 20
HEAVY = 20_000_000_000
LIGHT = 20_000_000_000
VMEM = pl.BlockSpec(memory_space=pltpu.VMEM)


def swapped(value, axis, step):
    count = lax.axis_size(axis)
    return lax.ppermute(value, axis, [(source, source ^ step) for source in range(count)])


def in_vmem(value):
    return pltpu.with_memory_space_constraint(value, pltpu.VMEM)


def in_hbm(value):
    return pltpu.with_memory_space_constraint(value, pltpu.HBM)


def kernel_call(kernel, out_shape, in_specs, flops, limit, scratch=(), aliases=None):
    return pl.pallas_call(
        kernel,
        out_shape=out_shape,
        in_specs=in_specs,
        out_specs=jax.tree.map(lambda _: VMEM, out_shape),
        scratch_shapes=list(scratch),
        input_output_aliases=aliases or {},
        cost_estimate=pl.CostEstimate(flops=flops, bytes_accessed=0, transcendentals=0),
        compiler_params=pltpu.CompilerParams(vmem_limit_bytes=limit),
    )


def three_parts(value):
    high = value.astype(jnp.bfloat16).astype(jnp.float32)
    rest = value - high
    middle = rest.astype(jnp.bfloat16).astype(jnp.float32)
    return (high, middle, rest - middle)


def attend(step, group_rows, q_ref, key_ref, value_ref, key_table, value_table, bias_ref, out_ref):
    req_dev, rows_dev, head_dim = q_ref.shape
    head = (lax.axis_index("seq") ^ step) * rows_dev // group_rows
    heads = key_ref.shape[1]
    reqs = range(req_dev)
    raw = [
        lax.dot_general(
            q_ref[req],
            key_ref[req, head],
            (((1,), (1,)), ((), ())),
            preferred_element_type=jnp.float32,
        )
        for req in reqs
    ]
    copies = rows_dev // bias_ref.shape[1]
    masked = [
        raw[req] * key_table[pl.ds(req * heads + head, 1), :]
        + jnp.concatenate([bias_ref[req]] * copies, axis=0)
        for req in reqs
    ]
    top = [jnp.max(part, axis=1, keepdims=True) for part in masked]
    weights = [jnp.exp2(part - high) for part, high in zip(masked, top)]
    total = [
        jnp.where(high > 0.5 * NEG_FLOOR, jnp.sum(part, axis=1, keepdims=True), 0.0)
        for part, high in zip(weights, top)
    ]
    scaled = [
        (weights[req] * value_table[pl.ds(req * heads + head, 1), :]).astype(jnp.bfloat16)
        for req in reqs
    ]
    acc = [
        jnp.dot(scaled[req], value_ref[req, head], preferred_element_type=jnp.float32)
        for req in reqs
    ]
    rows = req_dev * rows_dev
    stat_lane = lax.broadcasted_iota(jnp.int32, (rows, head_dim), 1)
    stats = jnp.zeros((rows, head_dim), jnp.float32)
    pieces = three_parts(jnp.concatenate(top, axis=0)) + three_parts(jnp.concatenate(total, axis=0))
    for at, part in enumerate(pieces):
        stats = jnp.where(stat_lane == at, part, stats)
    out_ref[:rows, :] = jnp.concatenate(acc, axis=0).astype(jnp.bfloat16)
    out_ref[rows:, :] = jnp.transpose(stats)[:STAT_ROWS].astype(jnp.bfloat16)


def first_kernel(group_rows, *refs):
    given, refs = refs[:8], refs[8:]
    key_ref, value_ref, key_table, value_table, bias_ref, out_ref = refs[:6]
    q_ref, ctx, start, depth, key_scale, value_scale, sems = refs[6:]
    targets = (q_ref, ctx, start, depth, key_scale, value_scale, key_ref, value_ref)
    copies = [
        pltpu.make_async_copy(source, target, sems.at[at])
        for at, (source, target) in enumerate(zip(given, targets))
    ]
    for copy in copies:
        copy.start()
    req_dev, rows_dev, head_dim = q_ref.shape
    heads, kv_rows = key_ref.shape[1:3]
    blocks = key_scale.shape[2]
    width = kv_rows // blocks
    drafts = depth.shape[1]
    seq_count = lax.axis_size("seq")
    here = lax.axis_index("seq")
    lane = lax.broadcasted_iota(jnp.int32, (1, kv_rows), 1)
    tall = bias_ref.shape[1]
    draft_of = lax.broadcasted_iota(jnp.int32, (tall, kv_rows), 0) % drafts
    for copy in copies[1:6]:
        copy.wait()
    factor = math.log2(math.e) / math.sqrt(head_dim)
    for req in range(req_dev):
        for head in range(heads):
            for scale, table, by in ((key_scale, key_table, factor), (value_scale, value_table, 1.0)):
                found = jnp.full((1, kv_rows), scale[req, head, 0] * by, jnp.float32)
                for block in range(1, blocks):
                    found = jnp.where(lane >= block * width, scale[req, head, block] * by, found)
                table[req * heads + head : req * heads + head + 1, :] = found
        first = jnp.where(here >= start[req], here - start[req], here - start[req] + seq_count)
        limit = jnp.full((tall, kv_rows), depth[req, 0], jnp.int32)
        for draft in range(1, drafts):
            limit = jnp.where(draft_of == draft, depth[req, draft], limit)
        limit = limit + (ctx[req] - drafts - first * kv_rows)
        bias_ref[req] = jnp.where(lane <= limit, 0.0, NEG_FLOOR)
    copies[0].wait()
    copies[6].wait()
    copies[7].wait()
    attend(0, group_rows, q_ref, key_ref, value_ref, key_table, value_table, bias_ref, out_ref)


def attend_kernel(steps, group_rows, *refs):
    count = len(steps)
    for step, q_ref, out_ref in zip(steps, refs[:count], refs[count + 5 :]):
        attend(step, group_rows, q_ref, *refs[count : count + 5], out_ref)


def merge_kernel(req_dev, rows_dev, drafts, *refs):
    part_refs = refs[:-3]
    out_ref, held, ordered = refs[-3:]
    rows = req_dev * rows_dev
    heads = rows_dev // drafts
    head_count = lax.axis_size("head")
    share = drafts // head_count
    mine = lax.axis_index("head")
    stats = [ref[rows:, :].astype(jnp.float32) for ref in part_refs]
    tops = [stat[0:1] + stat[1:2] + stat[2:3] for stat in stats]
    totals = [stat[3:4] + stat[4:5] + stat[5:6] for stat in stats]
    top = functools.reduce(jnp.maximum, tops)
    factors = [jnp.exp2(value - top) for value in tops]
    total = sum(value * factor for value, factor in zip(totals, factors))
    lanes = top.shape[1]
    which = lax.broadcasted_iota(jnp.int32, (lanes, lanes), 0)
    table = jnp.zeros((lanes, lanes), jnp.float32)
    for at, factor in enumerate(factors):
        table = jnp.where(which == at, factor / total, table)
    turned = jnp.transpose(table)
    merged = sum(
        ref[:rows, :].astype(jnp.float32) * turned[:, at : at + 1]
        for at, ref in enumerate(part_refs)
    )
    held[...] = merged
    for req in range(req_dev):
        for draft in range(drafts):
            taken = held[pl.ds(req * rows_dev + draft, heads, stride=drafts), :]
            place = (draft // share) ^ mine
            row = (place * share + draft % share) * req_dev + req
            ordered[pl.ds(row, heads, stride=drafts * req_dev), :] = taken
    out_ref[...] = ordered[...].astype(jnp.bfloat16)


def project_kernel(steps, first, *refs):
    count = len(steps)
    x_refs = refs[:count]
    weight_ref = refs[count]
    before = None if first else refs[count + 1]
    out_refs = refs[count + 1 if first else count + 2 :]
    rows, head_dim = x_refs[0].shape
    here = lax.axis_index("seq")
    depth = weight_ref.shape[0] // lax.axis_size("seq")
    heads = depth // head_dim
    lines = rows // heads
    x_parts = [
        jnp.concatenate(
            [ref[head * lines : (head + 1) * lines, :] for head in range(heads)], axis=1
        )
        for ref in x_refs
    ]
    wide = weight_ref.shape[1]
    cut = min(wide, 512)
    for column in range(0, wide, cut):
        spot = slice(column, column + cut)
        found = None if first else before[:, spot]
        for step, part in zip(steps, x_parts):
            start = pl.multiple_of((here ^ step) * depth, depth)
            product = jnp.dot(
                part, weight_ref[pl.ds(start, depth), spot], preferred_element_type=jnp.float32
            )
            found = product if found is None else found + product
        tall = out_refs[0].shape[0]
        for piece, out_ref in enumerate(out_refs):
            out_ref[:, spot] = found[piece * tall : (piece + 1) * tall].astype(out_ref.dtype)


def sum_kernel(*refs):
    out_ref = refs[-1]
    total = refs[0][...].astype(jnp.float32)
    for ref in refs[1:-1]:
        total = total + ref[...].astype(jnp.float32)
    out_ref[...] = total.astype(out_ref.dtype).reshape(out_ref.shape)


def with_kernels(
    queries,
    key_codes,
    key_scale,
    value_codes,
    value_scale,
    out_weight,
    ctx_len,
    start_shard,
    draft_depth,
):
    seq_count = lax.axis_size("seq")
    head_count = lax.axis_size("head")
    req_dev, rows_dev, head_dim = queries.shape
    group_rows = seq_count * rows_dev // key_codes.shape[1]
    drafts = draft_depth.shape[1]
    rows = req_dev * rows_dev
    wide = out_weight.shape[1]
    others = range(1, seq_count)
    kv_heads, kv_rows = key_codes.shape[1:3]
    tall = 2 * drafts
    payload = pltpu.VMEM((rows + STAT_ROWS, head_dim), jnp.bfloat16)
    given = (
        queries,
        ctx_len,
        start_shard,
        draft_depth,
        key_scale,
        value_scale,
        key_codes,
        value_codes,
    )
    arrived = [swapped(queries, "seq", step) for step in others]
    *tables, own = kernel_call(
        functools.partial(first_kernel, group_rows),
        [
            pltpu.VMEM(key_codes.shape, key_codes.dtype),
            pltpu.VMEM(value_codes.shape, value_codes.dtype),
            pltpu.VMEM((req_dev * kv_heads, kv_rows), jnp.float32),
            pltpu.VMEM((req_dev * kv_heads, kv_rows), jnp.float32),
            pltpu.VMEM((req_dev, tall, kv_rows), jnp.float32),
            payload,
        ],
        [pl.BlockSpec(memory_space=pltpu.HBM)] * len(given),
        HEAVY,
        8 * MIB,
        [pltpu.VMEM(queries.shape, queries.dtype)]
        + [pltpu.SMEM(part.shape, part.dtype) for part in given[1:6]]
        + [pltpu.SemaphoreType.DMA((len(given),))],
    )(*map(in_hbm, given))
    partials = kernel_call(
        functools.partial(attend_kernel, tuple(others), group_rows),
        [payload] * len(others),
        [VMEM] * (len(others) + len(tables)),
        LIGHT,
        8 * MIB,
    )(*arrived, *tables)
    returned = [swapped(part, "seq", step) for step, part in zip(others, partials)]
    finished = kernel_call(
        functools.partial(merge_kernel, req_dev, rows_dev, drafts),
        pltpu.VMEM((rows, head_dim), jnp.bfloat16),
        [VMEM] * seq_count,
        LIGHT,
        4 * MIB,
        [pltpu.VMEM((rows, head_dim), jnp.float32)] * 2,
    )(own, *returned)
    gathered = [swapped(finished, "seq", step) for step in others]
    lines = drafts * req_dev
    shares = kernel_call(
        functools.partial(project_kernel, tuple(range(seq_count)), True),
        [pltpu.VMEM((lines // head_count, wide), jnp.bfloat16)] * head_count,
        [VMEM] * (seq_count + 1),
        LIGHT,
        8 * MIB,
    )(finished, *gathered, in_vmem(out_weight))
    summed = [swapped(shares[step], "head", step) for step in range(head_count - 1, 0, -1)]
    return kernel_call(
        sum_kernel,
        jax.ShapeDtypeStruct((drafts // head_count, req_dev, wide), jnp.bfloat16),
        [VMEM] * head_count,
        LIGHT,
        4 * MIB,
    )(shares[0], *summed)


def passed_along(value, axis, steps):
    count = lax.axis_size(axis)
    pairs = [(source, (source + steps) % count) for source in range(count)]
    return lax.ppermute(value, axis, pairs)


def combine_state(first, second):
    top = jnp.maximum(first[0], second[0])
    early = jnp.exp(first[0] - top)
    later = jnp.exp(second[0] - top)
    return (
        top,
        first[1] * early + second[1] * later,
        first[2] * early[..., None] + second[2] * later[..., None],
    )


def shard_partial(block_q, key_block, key_tok, value_block, value_tok, positions, limits):
    raw = jnp.einsum("rhqd,rhkd->rhqk", block_q, key_block, preferred_element_type=jnp.float32)
    scores = raw * (key_tok[:, :, None, :] * (1.0 / math.sqrt(HD)))
    visible = positions[:, None, None, :] <= limits[:, None, :, None]
    masked = jnp.where(visible, scores, NEG_FLOOR)
    top = jnp.max(masked, axis=3)
    weights = jnp.where(visible, jnp.exp(masked - top[..., None]), 0.0)
    total = jnp.sum(weights, axis=3)
    scaled = (weights * value_tok[:, :, None, :]).astype(jnp.bfloat16)
    acc = jnp.einsum("rhqk,rhkd->rhqd", scaled, value_block, preferred_element_type=jnp.float32)
    return (top, total, acc)


def round_the_ring(
    queries,
    key_codes,
    key_scale,
    value_codes,
    value_scale,
    out_weight,
    ctx_len,
    start_shard,
    draft_depth,
):
    seq_count = lax.axis_size("seq")
    here = lax.axis_index("seq")
    req_dev, rows_dev, head_dim = queries.shape
    kv_rows = key_codes.shape[2]
    group_rows = QHEADS // KVH * DRAFT
    key_tok = jnp.repeat(key_scale, BLK, axis=2)
    value_tok = jnp.repeat(value_scale, BLK, axis=2)
    offsets = jnp.mod(here - start_shard, seq_count)
    positions = offsets[:, None] * kv_rows + jnp.arange(kv_rows, dtype=jnp.int32)[None, :]
    base_limit = ctx_len - DRAFT
    draft_ids = jnp.arange(DRAFT, dtype=jnp.int32)

    def row_limits(first, count):
        draft_of = (first + jnp.arange(count, dtype=jnp.int32)) % DRAFT
        pick = (draft_of[:, None] == draft_ids[None, :]).astype(jnp.int32)
        return base_limit[:, None] + jnp.sum(draft_depth[:, None, :] * pick[None], axis=2)

    def turn(step, carry):
        block_q, top, total, acc = carry
        anchor = jnp.mod(here - step, seq_count)
        first = anchor * rows_dev
        head_pick = first // group_rows
        key_block = lax.dynamic_slice_in_dim(key_codes, head_pick, 1, 1)
        value_block = lax.dynamic_slice_in_dim(value_codes, head_pick, 1, 1)
        key_sel = lax.dynamic_slice_in_dim(key_tok, head_pick, 1, 1)
        value_sel = lax.dynamic_slice_in_dim(value_tok, head_pick, 1, 1)
        part = shard_partial(
            block_q[:, None],
            key_block,
            key_sel,
            value_block,
            value_sel,
            positions,
            row_limits(first, rows_dev),
        )
        merged = combine_state((top, total, acc), (part[0][:, 0], part[1][:, 0], part[2][:, 0]))
        moved = passed_along(
            (block_q.astype(jnp.float32), merged[0], merged[1], merged[2]), "seq", 1
        )
        return (moved[0].astype(jnp.bfloat16), moved[1], moved[2], moved[3])

    start_state = (
        queries,
        jnp.full((req_dev, rows_dev), NEG_FLOOR, jnp.float32),
        jnp.zeros((req_dev, rows_dev), jnp.float32),
        jnp.zeros((req_dev, rows_dev, head_dim), jnp.float32),
    )
    final = lax.fori_loop(0, seq_count, turn, start_state)
    attention = (final[3] / final[2][..., None]).astype(jnp.bfloat16)
    gathered = lax.all_gather(attention, "seq", axis=1, tiled=True)
    heads = gathered.shape[1] // DRAFT
    arranged = gathered.reshape(req_dev, heads, DRAFT, head_dim)
    width_dev = out_weight.shape[1]
    flat = jnp.transpose(arranged, (2, 0, 1, 3)).reshape(DRAFT * req_dev, heads * head_dim)
    result = jnp.dot(flat, out_weight, preferred_element_type=jnp.float32)
    summed = lax.psum_scatter(
        result.reshape(DRAFT, req_dev, width_dev), "head", scatter_dimension=0, tiled=True
    )
    return summed.astype(jnp.bfloat16)


def on_device(*arrays):
    queries, key_codes = arrays[:2]
    seq_count, head_count = lax.axis_size("seq"), lax.axis_size("head")
    req_dev, rows_dev, head_dim = queries.shape
    paired = all(count & (count - 1) == 0 for count in (seq_count, head_count))
    tiled = req_dev * rows_dev == head_dim and rows_dev % (2 * DRAFT) == 0
    whole = seq_count * rows_dev // key_codes.shape[1] % rows_dev == 0
    if paired and tiled and whole and DRAFT % head_count == 0:
        return with_kernels(*arrays)
    return round_the_ring(*arrays)


def solution(mesh):
    placed = (
        P("req", ("head", "seq"), None),
        P("req", "head", "seq", None),
        P("req", "head", "seq"),
        P("req", "head", "seq", None),
        P("req", "head", "seq"),
        P("head", "seq"),
        P("req"),
        P("req"),
        P("req", None),
    )
    return jax.shard_map(
        on_device, mesh=mesh, in_specs=placed, out_specs=P("head", "req", "seq"), check_vma=False
    )
```

```python
import functools
import math

import jax
import jax.numpy as jnp
from jax import lax
from jax.experimental import pallas as pl
from jax.experimental.pallas import tpu as pltpu
from jax.sharding import PartitionSpec as P

QHEADS = 128
KVH = 8
HD = 128
DRAFT = 4
BLK = 64

NEG_FLOOR = -1e30
STAT_ROWS = 16
MIB = 1 << 20
HEAVY = 20_000_000_000
LIGHT = 20_000_000_000
VMEM = pl.BlockSpec(memory_space=pltpu.VMEM)


def swapped(value, axis, step):
    count = lax.axis_size(axis)
    return lax.ppermute(value, axis, [(source, source ^ step) for source in range(count)])


def in_vmem(value):
    return pltpu.with_memory_space_constraint(value, pltpu.VMEM)


def in_hbm(value):
    return pltpu.with_memory_space_constraint(value, pltpu.HBM)


def kernel_call(kernel, out_shape, in_specs, flops, limit, scratch=(), aliases=None):
    return pl.pallas_call(
        kernel,
        out_shape=out_shape,
        in_specs=in_specs,
        out_specs=jax.tree.map(lambda _: VMEM, out_shape),
        scratch_shapes=list(scratch),
        input_output_aliases=aliases or {},
        cost_estimate=pl.CostEstimate(flops=flops, bytes_accessed=0, transcendentals=0),
        compiler_params=pltpu.CompilerParams(vmem_limit_bytes=limit),
    )


def three_parts(value):
    high = value.astype(jnp.bfloat16).astype(jnp.float32)
    rest = value - high
    middle = rest.astype(jnp.bfloat16).astype(jnp.float32)
    return (high, middle, rest - middle)


def attend(step, group_rows, q_ref, key_ref, value_ref, key_table, value_table, bias_ref, out_ref):
    req_dev, rows_dev, head_dim = q_ref.shape
    head = (lax.axis_index("seq") ^ step) * rows_dev // group_rows
    heads = key_ref.shape[1]
    reqs = range(req_dev)
    raw = [
        lax.dot_general(
            q_ref[req],
            key_ref[req, head],
            (((1,), (1,)), ((), ())),
            preferred_element_type=jnp.float32,
        )
        for req in reqs
    ]
    copies = rows_dev // bias_ref.shape[1]
    masked = [
        raw[req] * key_table[pl.ds(req * heads + head, 1), :]
        + jnp.concatenate([bias_ref[req]] * copies, axis=0)
        for req in reqs
    ]
    top = [jnp.max(part, axis=1, keepdims=True) for part in masked]
    weights = [jnp.exp2(part - high) for part, high in zip(masked, top)]
    total = [
        jnp.where(high > 0.5 * NEG_FLOOR, jnp.sum(part, axis=1, keepdims=True), 0.0)
        for part, high in zip(weights, top)
    ]
    scaled = [
        (weights[req] * value_table[pl.ds(req * heads + head, 1), :]).astype(jnp.bfloat16)
        for req in reqs
    ]
    acc = [
        jnp.dot(scaled[req], value_ref[req, head], preferred_element_type=jnp.float32)
        for req in reqs
    ]
    rows = req_dev * rows_dev
    stat_lane = lax.broadcasted_iota(jnp.int32, (rows, head_dim), 1)
    stats = jnp.zeros((rows, head_dim), jnp.float32)
    pieces = three_parts(jnp.concatenate(top, axis=0)) + three_parts(jnp.concatenate(total, axis=0))
    for at, part in enumerate(pieces):
        stats = jnp.where(stat_lane == at, part, stats)
    out_ref[:rows, :] = jnp.concatenate(acc, axis=0).astype(jnp.bfloat16)
    out_ref[rows:, :] = jnp.transpose(stats)[:STAT_ROWS].astype(jnp.bfloat16)


def prepare_kernel(head_dim, *refs):
    given, refs = refs[:7], refs[7:]
    key_ref, value_ref, key_table, value_table, bias_ref = refs[:5]
    ctx, start, depth, key_scale, value_scale, sems = refs[5:]
    targets = (ctx, start, depth, key_scale, value_scale, key_ref, value_ref)
    copies = [
        pltpu.make_async_copy(source, target, sems.at[at])
        for at, (source, target) in enumerate(zip(given, targets))
    ]
    for copy in copies:
        copy.start()
    req_dev, heads, kv_rows = key_ref.shape[:3]
    blocks = key_scale.shape[2]
    width = kv_rows // blocks
    drafts = depth.shape[1]
    seq_count = lax.axis_size("seq")
    here = lax.axis_index("seq")
    lane = lax.broadcasted_iota(jnp.int32, (1, kv_rows), 1)
    tall = bias_ref.shape[1]
    draft_of = lax.broadcasted_iota(jnp.int32, (tall, kv_rows), 0) % drafts
    for copy in copies[:5]:
        copy.wait()
    factor = math.log2(math.e) / math.sqrt(head_dim)
    for req in range(req_dev):
        for head in range(heads):
            for scale, table, by in ((key_scale, key_table, factor), (value_scale, value_table, 1.0)):
                found = jnp.full((1, kv_rows), scale[req, head, 0] * by, jnp.float32)
                for block in range(1, blocks):
                    found = jnp.where(lane >= block * width, scale[req, head, block] * by, found)
                table[req * heads + head : req * heads + head + 1, :] = found
        first = jnp.where(here >= start[req], here - start[req], here - start[req] + seq_count)
        limit = jnp.full((tall, kv_rows), depth[req, 0], jnp.int32)
        for draft in range(1, drafts):
            limit = jnp.where(draft_of == draft, depth[req, draft], limit)
        limit = limit + (ctx[req] - drafts - first * kv_rows)
        bias_ref[req] = jnp.where(lane <= limit, 0.0, NEG_FLOOR)
    for copy in copies[5:]:
        copy.wait()


def attend_kernel(steps, group_rows, *refs):
    count = len(steps)
    for step, q_ref, out_ref in zip(steps, refs[:count], refs[count + 5 :]):
        attend(step, group_rows, q_ref, *refs[count : count + 5], out_ref)


def merge_kernel(req_dev, rows_dev, drafts, *refs):
    part_refs = refs[:-3]
    out_ref, held, ordered = refs[-3:]
    rows = req_dev * rows_dev
    heads = rows_dev // drafts
    head_count = lax.axis_size("head")
    share = drafts // head_count
    mine = lax.axis_index("head")
    stats = [ref[rows:, :].astype(jnp.float32) for ref in part_refs]
    tops = [stat[0:1] + stat[1:2] + stat[2:3] for stat in stats]
    totals = [stat[3:4] + stat[4:5] + stat[5:6] for stat in stats]
    top = functools.reduce(jnp.maximum, tops)
    factors = [jnp.exp2(value - top) for value in tops]
    total = sum(value * factor for value, factor in zip(totals, factors))
    lanes = top.shape[1]
    which = lax.broadcasted_iota(jnp.int32, (lanes, lanes), 0)
    table = jnp.zeros((lanes, lanes), jnp.float32)
    for at, factor in enumerate(factors):
        table = jnp.where(which == at, factor / total, table)
    turned = jnp.transpose(table)
    merged = sum(
        ref[:rows, :].astype(jnp.float32) * turned[:, at : at + 1]
        for at, ref in enumerate(part_refs)
    )
    held[...] = merged
    for req in range(req_dev):
        for draft in range(drafts):
            taken = held[pl.ds(req * rows_dev + draft, heads, stride=drafts), :]
            place = (draft // share) ^ mine
            row = (place * share + draft % share) * req_dev + req
            ordered[pl.ds(row, heads, stride=drafts * req_dev), :] = taken
    out_ref[...] = ordered[...].astype(jnp.bfloat16)


def project_parts(ref, depth):
    head_dim = ref.shape[1]
    heads = depth // head_dim
    lines = ref.shape[0] // heads
    return jnp.concatenate(
        [ref[head * lines : (head + 1) * lines, :] for head in range(heads)], axis=1
    )


def project_kernel(steps, *refs):
    count = len(steps)
    x_refs = refs[:count]
    weight_ref = refs[count]
    out_refs = refs[count + 1 :]
    here = lax.axis_index("seq")
    depth = weight_ref.shape[0] // lax.axis_size("seq")
    x_parts = [project_parts(ref, depth) for ref in x_refs]
    wide = weight_ref.shape[1]
    cut = min(wide, 512)
    tall = out_refs[0].shape[0]
    for column in range(0, wide, cut):
        spot = slice(column, column + cut)
        found = jnp.zeros((tall * len(out_refs), cut), jnp.float32)
        for step, part in zip(steps, x_parts):
            start = pl.multiple_of((here ^ step) * depth, depth)
            found = found + jnp.dot(
                part, weight_ref[pl.ds(start, depth), spot], preferred_element_type=jnp.float32
            )
        for piece, out_ref in enumerate(out_refs):
            out_ref[:, spot] = found[piece * tall : (piece + 1) * tall].astype(out_ref.dtype)


def sum_kernel(*refs):
    out_ref = refs[-1]
    total = refs[0][...].astype(jnp.float32)
    for ref in refs[1:-1]:
        total = total + ref[...].astype(jnp.float32)
    out_ref[...] = total.astype(out_ref.dtype).reshape(out_ref.shape)


def with_kernels(
    queries,
    key_codes,
    key_scale,
    value_codes,
    value_scale,
    out_weight,
    ctx_len,
    start_shard,
    draft_depth,
):
    seq_count = lax.axis_size("seq")
    head_count = lax.axis_size("head")
    req_dev, rows_dev, head_dim = queries.shape
    group_rows = seq_count * rows_dev // key_codes.shape[1]
    drafts = draft_depth.shape[1]
    rows = req_dev * rows_dev
    wide = out_weight.shape[1]
    others = range(1, seq_count)
    kv_heads, kv_rows = key_codes.shape[1:3]
    tall = 2 * drafts
    payload = pltpu.VMEM((rows + STAT_ROWS, head_dim), jnp.bfloat16)
    given = (
        ctx_len,
        start_shard,
        draft_depth,
        key_scale,
        value_scale,
        key_codes,
        value_codes,
    )
    tables = kernel_call(
        functools.partial(prepare_kernel, head_dim),
        [
            pltpu.VMEM(key_codes.shape, key_codes.dtype),
            pltpu.VMEM(value_codes.shape, value_codes.dtype),
            pltpu.VMEM((req_dev * kv_heads, kv_rows), jnp.float32),
            pltpu.VMEM((req_dev * kv_heads, kv_rows), jnp.float32),
            pltpu.VMEM((req_dev, tall, kv_rows), jnp.float32),
        ],
        [pl.BlockSpec(memory_space=pltpu.HBM)] * len(given),
        HEAVY,
        8 * MIB,
        [pltpu.SMEM(part.shape, part.dtype) for part in given[:5]]
        + [pltpu.SemaphoreType.DMA((len(given),))],
    )(*map(in_hbm, given))

    def partial(step, block):
        return kernel_call(
            functools.partial(attend_kernel, (step,), group_rows),
            payload,
            [VMEM] * (1 + len(tables)),
            LIGHT,
            4 * MIB,
        )(block, *tables)

    arrived = [swapped(queries, "seq", step) for step in others]
    partials = [partial(step, block) for step, block in zip(others, arrived)]
    own = partial(0, queries)
    returned = [swapped(part, "seq", step) for step, part in zip(others, partials)]
    finished = kernel_call(
        functools.partial(merge_kernel, req_dev, rows_dev, drafts),
        pltpu.VMEM((rows, head_dim), jnp.bfloat16),
        [VMEM] * seq_count,
        LIGHT,
        4 * MIB,
        [pltpu.VMEM((rows, head_dim), jnp.float32)] * 2,
    )(own, *returned)
    gathered = [swapped(finished, "seq", step) for step in others]
    lines = drafts * req_dev
    shares = kernel_call(
        functools.partial(project_kernel, tuple(range(seq_count))),
        [pltpu.VMEM((lines // head_count, wide), jnp.bfloat16)] * head_count,
        [VMEM] * (seq_count + 1),
        LIGHT,
        8 * MIB,
    )(finished, *gathered, in_vmem(out_weight))
    summed = [swapped(shares[step], "head", step) for step in range(head_count - 1, 0, -1)]
    return kernel_call(
        sum_kernel,
        jax.ShapeDtypeStruct((drafts // head_count, req_dev, wide), jnp.bfloat16),
        [VMEM] * head_count,
        LIGHT,
        4 * MIB,
    )(shares[0], *summed)


def passed_along(value, axis, steps):
    count = lax.axis_size(axis)
    pairs = [(source, (source + steps) % count) for source in range(count)]
    return lax.ppermute(value, axis, pairs)


def combine_state(first, second):
    top = jnp.maximum(first[0], second[0])
    early = jnp.exp(first[0] - top)
    later = jnp.exp(second[0] - top)
    return (
        top,
        first[1] * early + second[1] * later,
        first[2] * early[..., None] + second[2] * later[..., None],
    )


def shard_partial(block_q, key_block, key_tok, value_block, value_tok, positions, limits):
    raw = jnp.einsum("rhqd,rhkd->rhqk", block_q, key_block, preferred_element_type=jnp.float32)
    scores = raw * (key_tok[:, :, None, :] * (1.0 / math.sqrt(HD)))
    visible = positions[:, None, None, :] <= limits[:, None, :, None]
    masked = jnp.where(visible, scores, NEG_FLOOR)
    top = jnp.max(masked, axis=3)
    weights = jnp.where(visible, jnp.exp(masked - top[..., None]), 0.0)
    total = jnp.sum(weights, axis=3)
    scaled = (weights * value_tok[:, :, None, :]).astype(jnp.bfloat16)
    acc = jnp.einsum("rhqk,rhkd->rhqd", scaled, value_block, preferred_element_type=jnp.float32)
    return (top, total, acc)


def round_the_ring(
    queries,
    key_codes,
    key_scale,
    value_codes,
    value_scale,
    out_weight,
    ctx_len,
    start_shard,
    draft_depth,
):
    seq_count = lax.axis_size("seq")
    here = lax.axis_index("seq")
    req_dev, rows_dev, head_dim = queries.shape
    kv_rows = key_codes.shape[2]
    group_rows = QHEADS // KVH * DRAFT
    key_tok = jnp.repeat(key_scale, BLK, axis=2)
    value_tok = jnp.repeat(value_scale, BLK, axis=2)
    offsets = jnp.mod(here - start_shard, seq_count)
    positions = offsets[:, None] * kv_rows + jnp.arange(kv_rows, dtype=jnp.int32)[None, :]
    base_limit = ctx_len - DRAFT
    draft_ids = jnp.arange(DRAFT, dtype=jnp.int32)

    def row_limits(first, count):
        draft_of = (first + jnp.arange(count, dtype=jnp.int32)) % DRAFT
        pick = (draft_of[:, None] == draft_ids[None, :]).astype(jnp.int32)
        return base_limit[:, None] + jnp.sum(draft_depth[:, None, :] * pick[None], axis=2)

    def turn(step, carry):
        block_q, top, total, acc = carry
        anchor = jnp.mod(here - step, seq_count)
        first = anchor * rows_dev
        head_pick = first // group_rows
        key_block = lax.dynamic_slice_in_dim(key_codes, head_pick, 1, 1)
        value_block = lax.dynamic_slice_in_dim(value_codes, head_pick, 1, 1)
        key_sel = lax.dynamic_slice_in_dim(key_tok, head_pick, 1, 1)
        value_sel = lax.dynamic_slice_in_dim(value_tok, head_pick, 1, 1)
        part = shard_partial(
            block_q[:, None],
            key_block,
            key_sel,
            value_block,
            value_sel,
            positions,
            row_limits(first, rows_dev),
        )
        merged = combine_state((top, total, acc), (part[0][:, 0], part[1][:, 0], part[2][:, 0]))
        moved = passed_along(
            (block_q.astype(jnp.float32), merged[0], merged[1], merged[2]), "seq", 1
        )
        return (moved[0].astype(jnp.bfloat16), moved[1], moved[2], moved[3])

    start_state = (
        queries,
        jnp.full((req_dev, rows_dev), NEG_FLOOR, jnp.float32),
        jnp.zeros((req_dev, rows_dev), jnp.float32),
        jnp.zeros((req_dev, rows_dev, head_dim), jnp.float32),
    )
    final = lax.fori_loop(0, seq_count, turn, start_state)
    attention = (final[3] / final[2][..., None]).astype(jnp.bfloat16)
    gathered = lax.all_gather(attention, "seq", axis=1, tiled=True)
    heads = gathered.shape[1] // DRAFT
    arranged = gathered.reshape(req_dev, heads, DRAFT, head_dim)
    width_dev = out_weight.shape[1]
    flat = jnp.transpose(arranged, (2, 0, 1, 3)).reshape(DRAFT * req_dev, heads * head_dim)
    result = jnp.dot(flat, out_weight, preferred_element_type=jnp.float32)
    summed = lax.psum_scatter(
        result.reshape(DRAFT, req_dev, width_dev), "head", scatter_dimension=0, tiled=True
    )
    return summed.astype(jnp.bfloat16)


def on_device(*arrays):
    queries, key_codes = arrays[:2]
    seq_count, head_count = lax.axis_size("seq"), lax.axis_size("head")
    req_dev, rows_dev, head_dim = queries.shape
    paired = all(count & (count - 1) == 0 for count in (seq_count, head_count))
    tiled = req_dev * rows_dev == head_dim and rows_dev % (2 * DRAFT) == 0
    whole = seq_count * rows_dev // key_codes.shape[1] % rows_dev == 0
    if paired and tiled and whole and DRAFT % head_count == 0:
        return with_kernels(*arrays)
    return round_the_ring(*arrays)


def solution(mesh):
    placed = (
        P("req", ("head", "seq"), None),
        P("req", "head", "seq", None),
        P("req", "head", "seq"),
        P("req", "head", "seq", None),
        P("req", "head", "seq"),
        P("head", "seq"),
        P("req"),
        P("req"),
        P("req", None),
    )
    return jax.shard_map(
        on_device, mesh=mesh, in_specs=placed, out_specs=P("head", "req", "seq"), check_vma=False
    )
```

```python
import functools
import math

import jax
import jax.numpy as jnp
from jax import lax
from jax.experimental import pallas as pl
from jax.experimental.pallas import tpu as pltpu
from jax.sharding import PartitionSpec as P

QHEADS = 128
KVH = 8
HD = 128
DRAFT = 4
BLK = 64

NEG_FLOOR = -1e30
STAT_ROWS = 16
MIB = 1 << 20
HEAVY = 20_000_000_000
LIGHT = 4_000_000_000
VMEM = pl.BlockSpec(memory_space=pltpu.VMEM)


def swapped(value, axis, step):
    count = lax.axis_size(axis)
    return lax.ppermute(value, axis, [(source, source ^ step) for source in range(count)])


def in_vmem(value):
    return pltpu.with_memory_space_constraint(value, pltpu.VMEM)


def in_hbm(value):
    return pltpu.with_memory_space_constraint(value, pltpu.HBM)


def kernel_call(kernel, out_shape, in_specs, flops, limit, scratch=(), aliases=None):
    return pl.pallas_call(
        kernel,
        out_shape=out_shape,
        in_specs=in_specs,
        out_specs=jax.tree.map(lambda _: VMEM, out_shape),
        scratch_shapes=list(scratch),
        input_output_aliases=aliases or {},
        cost_estimate=pl.CostEstimate(flops=flops, bytes_accessed=0, transcendentals=0),
        compiler_params=pltpu.CompilerParams(vmem_limit_bytes=limit),
    )


def three_parts(value):
    high = value.astype(jnp.bfloat16).astype(jnp.float32)
    rest = value - high
    middle = rest.astype(jnp.bfloat16).astype(jnp.float32)
    return (high, middle, rest - middle)


def attend(step, group_rows, q_ref, key_ref, value_ref, key_table, value_table, bias_ref, out_ref):
    req_dev, rows_dev, head_dim = q_ref.shape
    head = (lax.axis_index("seq") ^ step) * rows_dev // group_rows
    heads = key_ref.shape[1]
    reqs = range(req_dev)
    raw = [
        lax.dot_general(
            q_ref[req],
            key_ref[req, head],
            (((1,), (1,)), ((), ())),
            preferred_element_type=jnp.float32,
        )
        for req in reqs
    ]
    copies = rows_dev // bias_ref.shape[1]
    masked = [
        raw[req] * key_table[pl.ds(req * heads + head, 1), :]
        + jnp.concatenate([bias_ref[req]] * copies, axis=0)
        for req in reqs
    ]
    top = [jnp.max(part, axis=1, keepdims=True) for part in masked]
    weights = [jnp.exp2(part - high) for part, high in zip(masked, top)]
    total = [
        jnp.where(high > 0.5 * NEG_FLOOR, jnp.sum(part, axis=1, keepdims=True), 0.0)
        for part, high in zip(weights, top)
    ]
    scaled = [
        (weights[req] * value_table[pl.ds(req * heads + head, 1), :]).astype(jnp.bfloat16)
        for req in reqs
    ]
    acc = [
        jnp.dot(scaled[req], value_ref[req, head], preferred_element_type=jnp.float32)
        for req in reqs
    ]
    rows = req_dev * rows_dev
    stat_lane = lax.broadcasted_iota(jnp.int32, (rows, head_dim), 1)
    stats = jnp.zeros((rows, head_dim), jnp.float32)
    pieces = three_parts(jnp.concatenate(top, axis=0)) + three_parts(jnp.concatenate(total, axis=0))
    for at, part in enumerate(pieces):
        stats = jnp.where(stat_lane == at, part, stats)
    out_ref[:rows, :] = jnp.concatenate(acc, axis=0).astype(jnp.bfloat16)
    out_ref[rows:, :] = jnp.transpose(stats)[:STAT_ROWS].astype(jnp.bfloat16)


def prepare_kernel(head_dim, *refs):
    given, refs = refs[:7], refs[7:]
    key_ref, value_ref, key_table, value_table, bias_ref = refs[:5]
    ctx, start, depth, key_scale, value_scale, sems = refs[5:]
    targets = (ctx, start, depth, key_scale, value_scale, key_ref, value_ref)
    copies = [
        pltpu.make_async_copy(source, target, sems.at[at])
        for at, (source, target) in enumerate(zip(given, targets))
    ]
    for copy in copies:
        copy.start()
    req_dev, heads, kv_rows = key_ref.shape[:3]
    blocks = key_scale.shape[2]
    width = kv_rows // blocks
    drafts = depth.shape[1]
    seq_count = lax.axis_size("seq")
    here = lax.axis_index("seq")
    lane = lax.broadcasted_iota(jnp.int32, (1, kv_rows), 1)
    tall = bias_ref.shape[1]
    draft_of = lax.broadcasted_iota(jnp.int32, (tall, kv_rows), 0) % drafts
    for copy in copies[:5]:
        copy.wait()
    factor = math.log2(math.e) / math.sqrt(head_dim)
    for req in range(req_dev):
        for head in range(heads):
            for scale, table, by in ((key_scale, key_table, factor), (value_scale, value_table, 1.0)):
                found = jnp.full((1, kv_rows), scale[req, head, 0] * by, jnp.float32)
                for block in range(1, blocks):
                    found = jnp.where(lane >= block * width, scale[req, head, block] * by, found)
                table[req * heads + head : req * heads + head + 1, :] = found
        first = jnp.where(here >= start[req], here - start[req], here - start[req] + seq_count)
        limit = jnp.full((tall, kv_rows), depth[req, 0], jnp.int32)
        for draft in range(1, drafts):
            limit = jnp.where(draft_of == draft, depth[req, draft], limit)
        limit = limit + (ctx[req] - drafts - first * kv_rows)
        bias_ref[req] = jnp.where(lane <= limit, 0.0, NEG_FLOOR)
    for copy in copies[5:]:
        copy.wait()


def attend_kernel(steps, group_rows, *refs):
    count = len(steps)
    for step, q_ref, out_ref in zip(steps, refs[:count], refs[count + 5 :]):
        attend(step, group_rows, q_ref, *refs[count : count + 5], out_ref)


def kept_steps(count):
    return [step for step in range(count) if step.bit_count() % 2 == 0]


def stat_rows(count):
    return -(-6 * count // STAT_ROWS) * STAT_ROWS


def read_stats(ref, first):
    stats = ref[first:, :].astype(jnp.float32)
    return [
        (
            stats[at : at + 1] + stats[at + 1 : at + 2] + stats[at + 2 : at + 3],
            stats[at + 3 : at + 4] + stats[at + 4 : at + 5] + stats[at + 5 : at + 6],
        )
        for at in range(0, stats.shape[0] - 5, 6)
    ]


def combine_stats(stats):
    top = functools.reduce(jnp.maximum, [part[0] for part in stats])
    factors = [jnp.exp2(part[0] - top) for part in stats]
    total = sum(part[1] * factor for part, factor in zip(stats, factors))
    return top, total, factors


def as_columns(rows):
    lanes = rows[0].shape[1]
    which = lax.broadcasted_iota(jnp.int32, (lanes, lanes), 0)
    table = jnp.zeros((lanes, lanes), jnp.float32)
    for at, row in enumerate(rows):
        table = jnp.where(which == at, row, table)
    turned = jnp.transpose(table)
    return [turned[:, at : at + 1] for at in range(len(rows))]


def pair_kernel(rows, *refs):
    kept = (len(refs) - 1) // 2
    pairs = list(zip(refs[:kept], refs[kept : 2 * kept]))
    out_ref = refs[-1]
    found, columns = [], []
    for pair in pairs:
        top, total, factors = combine_stats([read_stats(ref, rows)[0] for ref in pair])
        found += [*three_parts(top), *three_parts(total)]
        columns += factors
    columns = as_columns(columns)
    merged = [
        sum(
            ref[:rows, :].astype(jnp.float32) * columns[2 * at + side]
            for side, ref in enumerate(pair)
        )
        for at, pair in enumerate(pairs)
    ]
    spare = out_ref.shape[0] - rows * kept - len(found)
    found.append(jnp.zeros((spare, out_ref.shape[1]), jnp.float32))
    for at, part in enumerate(merged):
        out_ref[at * rows : (at + 1) * rows, :] = part.astype(jnp.bfloat16)
    out_ref[rows * kept :, :] = jnp.concatenate(found, axis=0).astype(jnp.bfloat16)


def merge_kernel(req_dev, rows_dev, drafts, *refs):
    count = (len(refs) - 2) // 2
    part_refs, out_refs = refs[:count], refs[count : 2 * count]
    held, ordered = refs[2 * count :]
    rows = req_dev * rows_dev
    heads = rows_dev // drafts
    share = drafts // lax.axis_size("head")
    mine = lax.axis_index("head")
    kept = kept_steps(count)
    stats = [read_stats(ref, rows * len(kept)) for ref in part_refs]
    sources = [
        [(peer, kept.index(block ^ peer)) for peer in range(count) if block ^ peer in kept]
        for block in range(count)
    ]
    table = []
    for pieces in sources:
        top, total, factors = combine_stats([stats[peer][at] for peer, at in pieces])
        table += [factor / total for factor in factors]
    columns = iter(as_columns(table))
    for block, pieces in enumerate(sources):
        held[block] = sum(
            part_refs[peer][at * rows : (at + 1) * rows, :].astype(jnp.float32) * next(columns)
            for peer, at in pieces
        )
    for block in range(count):
        for req in range(req_dev):
            for draft in range(drafts):
                taken = held[block, pl.ds(req * rows_dev + draft, heads, stride=drafts), :]
                place = (draft // share) ^ mine
                row = (place * share + draft % share) * req_dev + req
                ordered[block, pl.ds(row, heads, stride=drafts * req_dev), :] = taken
    for block in range(count):
        out_refs[block][...] = ordered[block].astype(jnp.bfloat16)


def project_parts(ref, depth):
    head_dim = ref.shape[1]
    heads = depth // head_dim
    lines = ref.shape[0] // heads
    return jnp.concatenate(
        [ref[head * lines : (head + 1) * lines, :] for head in range(heads)], axis=1
    )


def project_kernel(steps, *refs):
    count = len(steps)
    x_refs = refs[:count]
    weight_ref = refs[count]
    out_refs = refs[count + 1 :]
    here = lax.axis_index("seq")
    depth = weight_ref.shape[0] // lax.axis_size("seq")
    x_parts = [project_parts(ref, depth) for ref in x_refs]
    wide = weight_ref.shape[1]
    cut = min(wide, 512)
    tall = out_refs[0].shape[0]
    for column in range(0, wide, cut):
        spot = slice(column, column + cut)
        found = jnp.zeros((tall * len(out_refs), cut), jnp.float32)
        for step, part in zip(steps, x_parts):
            start = pl.multiple_of((here ^ step) * depth, depth)
            found = found + jnp.dot(
                part, weight_ref[pl.ds(start, depth), spot], preferred_element_type=jnp.float32
            )
        for piece, out_ref in enumerate(out_refs):
            out_ref[:, spot] = found[piece * tall : (piece + 1) * tall].astype(out_ref.dtype)


def sum_kernel(*refs):
    out_ref = refs[-1]
    total = refs[0][...].astype(jnp.float32)
    for ref in refs[1:-1]:
        total = total + ref[...].astype(jnp.float32)
    out_ref[...] = total.astype(out_ref.dtype).reshape(out_ref.shape)


def with_kernels(
    queries,
    key_codes,
    key_scale,
    value_codes,
    value_scale,
    out_weight,
    ctx_len,
    start_shard,
    draft_depth,
):
    seq_count = lax.axis_size("seq")
    head_count = lax.axis_size("head")
    req_dev, rows_dev, head_dim = queries.shape
    group_rows = seq_count * rows_dev // key_codes.shape[1]
    drafts = draft_depth.shape[1]
    rows = req_dev * rows_dev
    wide = out_weight.shape[1]
    others = range(1, seq_count)
    kv_heads, kv_rows = key_codes.shape[1:3]
    tall = 2 * drafts
    payload = pltpu.VMEM((rows + STAT_ROWS, head_dim), jnp.bfloat16)
    given = (
        ctx_len,
        start_shard,
        draft_depth,
        key_scale,
        value_scale,
        key_codes,
        value_codes,
    )
    tables = kernel_call(
        functools.partial(prepare_kernel, head_dim),
        [
            pltpu.VMEM(key_codes.shape, key_codes.dtype),
            pltpu.VMEM(value_codes.shape, value_codes.dtype),
            pltpu.VMEM((req_dev * kv_heads, kv_rows), jnp.float32),
            pltpu.VMEM((req_dev * kv_heads, kv_rows), jnp.float32),
            pltpu.VMEM((req_dev, tall, kv_rows), jnp.float32),
        ],
        [pl.BlockSpec(memory_space=pltpu.HBM)] * len(given),
        HEAVY,
        8 * MIB,
        [pltpu.SMEM(part.shape, part.dtype) for part in given[:5]]
        + [pltpu.SemaphoreType.DMA((len(given),))],
    )(*map(in_hbm, given))

    def partial(step, block):
        return kernel_call(
            functools.partial(attend_kernel, (step,), group_rows),
            payload,
            [VMEM] * (1 + len(tables)),
            LIGHT,
            4 * MIB,
        )(block, *tables)

    arrived = [swapped(queries, "seq", step) for step in others]
    partials = [partial(step, block) for step, block in zip(others, arrived)]
    own = partial(0, queries)
    partials = dict(zip(others, partials)) | {0: own}
    kept = kept_steps(seq_count)
    returned = [swapped(partials[step ^ 1], "seq", 1) for step in kept]
    paired = kernel_call(
        functools.partial(pair_kernel, rows),
        pltpu.VMEM((rows * len(kept) + stat_rows(len(kept)), head_dim), jnp.bfloat16),
        [VMEM] * (2 * len(kept)),
        LIGHT,
        4 * MIB,
    )(*[partials[step] for step in kept], *returned)
    gathered = [swapped(paired, "seq", step) for step in others]
    finished = kernel_call(
        functools.partial(merge_kernel, req_dev, rows_dev, drafts),
        [pltpu.VMEM((rows, head_dim), jnp.bfloat16)] * seq_count,
        [VMEM] * seq_count,
        LIGHT,
        4 * MIB,
        [pltpu.VMEM((seq_count, rows, head_dim), jnp.float32)] * 2,
    )(paired, *gathered)
    lines = drafts * req_dev
    shares = kernel_call(
        functools.partial(project_kernel, tuple(range(seq_count))),
        [pltpu.VMEM((lines // head_count, wide), jnp.bfloat16)] * head_count,
        [VMEM] * (seq_count + 1),
        LIGHT,
        8 * MIB,
    )(*finished, in_vmem(out_weight))
    summed = [swapped(shares[step], "head", step) for step in range(head_count - 1, 0, -1)]
    return kernel_call(
        sum_kernel,
        jax.ShapeDtypeStruct((drafts // head_count, req_dev, wide), jnp.bfloat16),
        [VMEM] * head_count,
        LIGHT,
        4 * MIB,
    )(shares[0], *summed)


def passed_along(value, axis, steps):
    count = lax.axis_size(axis)
    pairs = [(source, (source + steps) % count) for source in range(count)]
    return lax.ppermute(value, axis, pairs)


def combine_state(first, second):
    top = jnp.maximum(first[0], second[0])
    early = jnp.exp(first[0] - top)
    later = jnp.exp(second[0] - top)
    return (
        top,
        first[1] * early + second[1] * later,
        first[2] * early[..., None] + second[2] * later[..., None],
    )


def shard_partial(block_q, key_block, key_tok, value_block, value_tok, positions, limits):
    raw = jnp.einsum("rhqd,rhkd->rhqk", block_q, key_block, preferred_element_type=jnp.float32)
    scores = raw * (key_tok[:, :, None, :] * (1.0 / math.sqrt(HD)))
    visible = positions[:, None, None, :] <= limits[:, None, :, None]
    masked = jnp.where(visible, scores, NEG_FLOOR)
    top = jnp.max(masked, axis=3)
    weights = jnp.where(visible, jnp.exp(masked - top[..., None]), 0.0)
    total = jnp.sum(weights, axis=3)
    scaled = (weights * value_tok[:, :, None, :]).astype(jnp.bfloat16)
    acc = jnp.einsum("rhqk,rhkd->rhqd", scaled, value_block, preferred_element_type=jnp.float32)
    return (top, total, acc)


def round_the_ring(
    queries,
    key_codes,
    key_scale,
    value_codes,
    value_scale,
    out_weight,
    ctx_len,
    start_shard,
    draft_depth,
):
    seq_count = lax.axis_size("seq")
    here = lax.axis_index("seq")
    req_dev, rows_dev, head_dim = queries.shape
    kv_rows = key_codes.shape[2]
    group_rows = QHEADS // KVH * DRAFT
    key_tok = jnp.repeat(key_scale, BLK, axis=2)
    value_tok = jnp.repeat(value_scale, BLK, axis=2)
    offsets = jnp.mod(here - start_shard, seq_count)
    positions = offsets[:, None] * kv_rows + jnp.arange(kv_rows, dtype=jnp.int32)[None, :]
    base_limit = ctx_len - DRAFT
    draft_ids = jnp.arange(DRAFT, dtype=jnp.int32)

    def row_limits(first, count):
        draft_of = (first + jnp.arange(count, dtype=jnp.int32)) % DRAFT
        pick = (draft_of[:, None] == draft_ids[None, :]).astype(jnp.int32)
        return base_limit[:, None] + jnp.sum(draft_depth[:, None, :] * pick[None], axis=2)

    def turn(step, carry):
        block_q, top, total, acc = carry
        anchor = jnp.mod(here - step, seq_count)
        first = anchor * rows_dev
        head_pick = first // group_rows
        key_block = lax.dynamic_slice_in_dim(key_codes, head_pick, 1, 1)
        value_block = lax.dynamic_slice_in_dim(value_codes, head_pick, 1, 1)
        key_sel = lax.dynamic_slice_in_dim(key_tok, head_pick, 1, 1)
        value_sel = lax.dynamic_slice_in_dim(value_tok, head_pick, 1, 1)
        part = shard_partial(
            block_q[:, None],
            key_block,
            key_sel,
            value_block,
            value_sel,
            positions,
            row_limits(first, rows_dev),
        )
        merged = combine_state((top, total, acc), (part[0][:, 0], part[1][:, 0], part[2][:, 0]))
        moved = passed_along(
            (block_q.astype(jnp.float32), merged[0], merged[1], merged[2]), "seq", 1
        )
        return (moved[0].astype(jnp.bfloat16), moved[1], moved[2], moved[3])

    start_state = (
        queries,
        jnp.full((req_dev, rows_dev), NEG_FLOOR, jnp.float32),
        jnp.zeros((req_dev, rows_dev), jnp.float32),
        jnp.zeros((req_dev, rows_dev, head_dim), jnp.float32),
    )
    final = lax.fori_loop(0, seq_count, turn, start_state)
    attention = (final[3] / final[2][..., None]).astype(jnp.bfloat16)
    gathered = lax.all_gather(attention, "seq", axis=1, tiled=True)
    heads = gathered.shape[1] // DRAFT
    arranged = gathered.reshape(req_dev, heads, DRAFT, head_dim)
    width_dev = out_weight.shape[1]
    flat = jnp.transpose(arranged, (2, 0, 1, 3)).reshape(DRAFT * req_dev, heads * head_dim)
    result = jnp.dot(flat, out_weight, preferred_element_type=jnp.float32)
    summed = lax.psum_scatter(
        result.reshape(DRAFT, req_dev, width_dev), "head", scatter_dimension=0, tiled=True
    )
    return summed.astype(jnp.bfloat16)


def on_device(*arrays):
    queries, key_codes = arrays[:2]
    seq_count, head_count = lax.axis_size("seq"), lax.axis_size("head")
    req_dev, rows_dev, head_dim = queries.shape
    paired = all(count & (count - 1) == 0 for count in (seq_count, head_count))
    tiled = req_dev * rows_dev == head_dim and rows_dev % (2 * DRAFT) == 0
    whole = seq_count * rows_dev // key_codes.shape[1] % rows_dev == 0
    if paired and tiled and whole and DRAFT % head_count == 0:
        return with_kernels(*arrays)
    return round_the_ring(*arrays)


def solution(mesh):
    placed = (
        P("req", ("head", "seq"), None),
        P("req", "head", "seq", None),
        P("req", "head", "seq"),
        P("req", "head", "seq", None),
        P("req", "head", "seq"),
        P("head", "seq"),
        P("req"),
        P("req"),
        P("req", None),
    )
    return jax.shard_map(
        on_device, mesh=mesh, in_specs=placed, out_specs=P("head", "req", "seq"), check_vma=False
    )
```

```python
import functools
import math

import jax
import jax.numpy as jnp
from jax import lax
from jax.experimental import pallas as pl
from jax.experimental.pallas import tpu as pltpu
from jax.sharding import PartitionSpec as P

QHEADS = 128
KVH = 8
HD = 128
DRAFT = 4
BLK = 64

NEG_FLOOR = -1e30
STAT_ROWS = 16
MIB = 1 << 20
HEAVY = 20_000_000_000
LIGHT = 4_000_000_000
VMEM = pl.BlockSpec(memory_space=pltpu.VMEM)


def swapped(value, axis, step):
    count = lax.axis_size(axis)
    return lax.ppermute(value, axis, [(source, source ^ step) for source in range(count)])


def in_vmem(value):
    return pltpu.with_memory_space_constraint(value, pltpu.VMEM)


def in_hbm(value):
    return pltpu.with_memory_space_constraint(value, pltpu.HBM)


def kernel_call(kernel, out_shape, in_specs, flops, limit, scratch=(), aliases=None):
    return pl.pallas_call(
        kernel,
        out_shape=out_shape,
        in_specs=in_specs,
        out_specs=jax.tree.map(lambda _: VMEM, out_shape),
        scratch_shapes=list(scratch),
        input_output_aliases=aliases or {},
        cost_estimate=pl.CostEstimate(flops=flops, bytes_accessed=0, transcendentals=0),
        compiler_params=pltpu.CompilerParams(vmem_limit_bytes=limit),
    )


def three_parts(value):
    high = value.astype(jnp.bfloat16).astype(jnp.float32)
    rest = value - high
    middle = rest.astype(jnp.bfloat16).astype(jnp.float32)
    return (high, middle, rest - middle)


def attend(step, group_rows, q_ref, key_ref, value_ref, key_table, value_table, bias_ref, out_ref):
    req_dev, rows_dev, head_dim = q_ref.shape
    head = (lax.axis_index("seq") ^ step) * rows_dev // group_rows
    heads = key_ref.shape[1]
    reqs = range(req_dev)
    raw = [
        lax.dot_general(
            q_ref[req],
            key_ref[req, head],
            (((1,), (1,)), ((), ())),
            preferred_element_type=jnp.float32,
        )
        for req in reqs
    ]
    copies = rows_dev // bias_ref.shape[1]
    masked = [
        raw[req] * key_table[pl.ds(req * heads + head, 1), :]
        + jnp.concatenate([bias_ref[req]] * copies, axis=0)
        for req in reqs
    ]
    top = [jnp.max(part, axis=1, keepdims=True) for part in masked]
    weights = [jnp.exp2(part - high) for part, high in zip(masked, top)]
    total = [
        jnp.where(high > 0.5 * NEG_FLOOR, jnp.sum(part, axis=1, keepdims=True), 0.0)
        for part, high in zip(weights, top)
    ]
    scaled = [
        (weights[req] * value_table[pl.ds(req * heads + head, 1), :]).astype(jnp.bfloat16)
        for req in reqs
    ]
    acc = [
        jnp.dot(scaled[req], value_ref[req, head], preferred_element_type=jnp.float32)
        for req in reqs
    ]
    rows = req_dev * rows_dev
    stat_lane = lax.broadcasted_iota(jnp.int32, (rows, head_dim), 1)
    stats = jnp.zeros((rows, head_dim), jnp.float32)
    pieces = three_parts(jnp.concatenate(top, axis=0)) + three_parts(jnp.concatenate(total, axis=0))
    for at, part in enumerate(pieces):
        stats = jnp.where(stat_lane == at, part, stats)
    out_ref[:rows, :] = jnp.concatenate(acc, axis=0).astype(jnp.bfloat16)
    out_ref[rows:, :] = jnp.transpose(stats)[:STAT_ROWS].astype(jnp.bfloat16)


def prepare_kernel(head_dim, *refs):
    given, refs = refs[:7], refs[7:]
    key_ref, value_ref, key_table, value_table, bias_ref = refs[:5]
    ctx, start, depth, key_scale, value_scale, sems = refs[5:]
    targets = (ctx, start, depth, key_scale, value_scale, key_ref, value_ref)
    copies = [
        pltpu.make_async_copy(source, target, sems.at[at])
        for at, (source, target) in enumerate(zip(given, targets))
    ]
    for copy in copies:
        copy.start()
    req_dev, heads, kv_rows = key_ref.shape[:3]
    blocks = key_scale.shape[2]
    width = kv_rows // blocks
    drafts = depth.shape[1]
    seq_count = lax.axis_size("seq")
    here = lax.axis_index("seq")
    lane = lax.broadcasted_iota(jnp.int32, (1, kv_rows), 1)
    tall = bias_ref.shape[1]
    draft_of = lax.broadcasted_iota(jnp.int32, (tall, kv_rows), 0) % drafts
    for copy in copies[:5]:
        copy.wait()
    factor = math.log2(math.e) / math.sqrt(head_dim)
    for req in range(req_dev):
        for head in range(heads):
            for scale, table, by in ((key_scale, key_table, factor), (value_scale, value_table, 1.0)):
                found = jnp.full((1, kv_rows), scale[req, head, 0] * by, jnp.float32)
                for block in range(1, blocks):
                    found = jnp.where(lane >= block * width, scale[req, head, block] * by, found)
                table[req * heads + head : req * heads + head + 1, :] = found
        first = jnp.where(here >= start[req], here - start[req], here - start[req] + seq_count)
        limit = jnp.full((tall, kv_rows), depth[req, 0], jnp.int32)
        for draft in range(1, drafts):
            limit = jnp.where(draft_of == draft, depth[req, draft], limit)
        limit = limit + (ctx[req] - drafts - first * kv_rows)
        bias_ref[req] = jnp.where(lane <= limit, 0.0, NEG_FLOOR)
    for copy in copies[5:]:
        copy.wait()


def attend_kernel(steps, group_rows, *refs):
    count = len(steps)
    for step, q_ref, out_ref in zip(steps, refs[:count], refs[count + 5 :]):
        attend(step, group_rows, q_ref, *refs[count : count + 5], out_ref)


def kept_steps(count):
    return [step for step in range(count) if step.bit_count() % 2 == 0]


def stat_rows(count):
    return -(-6 * count // STAT_ROWS) * STAT_ROWS


def read_stats(ref, first):
    stats = ref[first:, :].astype(jnp.float32)
    return [
        (
            stats[at : at + 1] + stats[at + 1 : at + 2] + stats[at + 2 : at + 3],
            stats[at + 3 : at + 4] + stats[at + 4 : at + 5] + stats[at + 5 : at + 6],
        )
        for at in range(0, stats.shape[0] - 5, 6)
    ]


def combine_stats(stats):
    top = functools.reduce(jnp.maximum, [part[0] for part in stats])
    factors = [jnp.exp2(part[0] - top) for part in stats]
    total = sum(part[1] * factor for part, factor in zip(stats, factors))
    return top, total, factors


def as_columns(rows):
    lanes = rows[0].shape[1]
    which = lax.broadcasted_iota(jnp.int32, (lanes, lanes), 0)
    table = jnp.zeros((lanes, lanes), jnp.float32)
    for at, row in enumerate(rows):
        table = jnp.where(which == at, row, table)
    turned = jnp.transpose(table)
    return [turned[:, at : at + 1] for at in range(len(rows))]


def pair_kernel(rows, *refs):
    kept = (len(refs) - 1) // 2
    pairs = list(zip(refs[:kept], refs[kept : 2 * kept]))
    out_ref = refs[-1]
    found, columns = [], []
    for pair in pairs:
        top, total, factors = combine_stats([read_stats(ref, rows)[0] for ref in pair])
        found += [*three_parts(top), *three_parts(total)]
        columns += factors
    columns = as_columns(columns)
    merged = [
        sum(
            ref[:rows, :].astype(jnp.float32) * columns[2 * at + side]
            for side, ref in enumerate(pair)
        )
        for at, pair in enumerate(pairs)
    ]
    spare = out_ref.shape[0] - rows * kept - len(found)
    found.append(jnp.zeros((spare, out_ref.shape[1]), jnp.float32))
    for at, part in enumerate(merged):
        out_ref[at * rows : (at + 1) * rows, :] = part.astype(jnp.bfloat16)
    out_ref[rows * kept :, :] = jnp.concatenate(found, axis=0).astype(jnp.bfloat16)


def merge_kernel(peers, blocks, kept, rows_dev, drafts, *refs):
    count = len(peers)
    part_refs, out_refs = refs[:count], refs[count : count + len(blocks)]
    held, ordered = refs[count + len(blocks) :]
    rows = held.shape[1]
    req_dev = rows // rows_dev
    heads = rows_dev // drafts
    share = drafts // lax.axis_size("head")
    mine = lax.axis_index("head")
    stats = [read_stats(ref, rows * len(kept)) for ref in part_refs]
    places = [[kept.index(block ^ peer) for peer in peers] for block in blocks]
    table = []
    for place in places:
        _, total, factors = combine_stats([stat[at] for stat, at in zip(stats, place)])
        table += [factor / total for factor in factors]
    columns = iter(as_columns(table))
    for block, place in enumerate(places):
        held[block] = sum(
            ref[at * rows : (at + 1) * rows, :].astype(jnp.float32) * next(columns)
            for ref, at in zip(part_refs, place)
        )
    for block in range(len(blocks)):
        for req in range(req_dev):
            for draft in range(drafts):
                taken = held[block, pl.ds(req * rows_dev + draft, heads, stride=drafts), :]
                place = (draft // share) ^ mine
                row = (place * share + draft % share) * req_dev + req
                ordered[block, pl.ds(row, heads, stride=drafts * req_dev), :] = taken
    for block in range(len(blocks)):
        out_refs[block][...] = ordered[block].astype(jnp.bfloat16)


def project_parts(ref, depth):
    head_dim = ref.shape[1]
    heads = depth // head_dim
    lines = ref.shape[0] // heads
    return jnp.concatenate(
        [ref[head * lines : (head + 1) * lines, :] for head in range(heads)], axis=1
    )


def project_kernel(steps, first, *refs):
    count = len(steps)
    x_refs = refs[:count]
    weight_ref = refs[count]
    before = None if first else refs[count + 1]
    out_refs = refs[count + 1 if first else count + 2 :]
    here = lax.axis_index("seq")
    depth = weight_ref.shape[0] // lax.axis_size("seq")
    x_parts = [project_parts(ref, depth) for ref in x_refs]
    wide = weight_ref.shape[1]
    cut = min(wide, 512)
    tall = out_refs[0].shape[0]
    for column in range(0, wide, cut):
        spot = slice(column, column + cut)
        found = None if first else before[:, spot]
        for step, part in zip(steps, x_parts):
            start = pl.multiple_of((here ^ step) * depth, depth)
            product = jnp.dot(
                part, weight_ref[pl.ds(start, depth), spot], preferred_element_type=jnp.float32
            )
            found = product if found is None else found + product
        for piece, out_ref in enumerate(out_refs):
            out_ref[:, spot] = found[piece * tall : (piece + 1) * tall].astype(out_ref.dtype)


def sum_kernel(*refs):
    out_ref = refs[-1]
    total = refs[0][...].astype(jnp.float32)
    for ref in refs[1:-1]:
        total = total + ref[...].astype(jnp.float32)
    out_ref[...] = total.astype(out_ref.dtype).reshape(out_ref.shape)


def with_kernels(
    queries,
    key_codes,
    key_scale,
    value_codes,
    value_scale,
    out_weight,
    ctx_len,
    start_shard,
    draft_depth,
):
    seq_count = lax.axis_size("seq")
    head_count = lax.axis_size("head")
    req_dev, rows_dev, head_dim = queries.shape
    group_rows = seq_count * rows_dev // key_codes.shape[1]
    drafts = draft_depth.shape[1]
    rows = req_dev * rows_dev
    wide = out_weight.shape[1]
    others = range(1, seq_count)
    kv_heads, kv_rows = key_codes.shape[1:3]
    tall = 2 * drafts
    payload = pltpu.VMEM((rows + STAT_ROWS, head_dim), jnp.bfloat16)
    given = (
        ctx_len,
        start_shard,
        draft_depth,
        key_scale,
        value_scale,
        key_codes,
        value_codes,
    )
    tables = kernel_call(
        functools.partial(prepare_kernel, head_dim),
        [
            pltpu.VMEM(key_codes.shape, key_codes.dtype),
            pltpu.VMEM(value_codes.shape, value_codes.dtype),
            pltpu.VMEM((req_dev * kv_heads, kv_rows), jnp.float32),
            pltpu.VMEM((req_dev * kv_heads, kv_rows), jnp.float32),
            pltpu.VMEM((req_dev, tall, kv_rows), jnp.float32),
        ],
        [pl.BlockSpec(memory_space=pltpu.HBM)] * len(given),
        HEAVY,
        8 * MIB,
        [pltpu.SMEM(part.shape, part.dtype) for part in given[:5]]
        + [pltpu.SemaphoreType.DMA((len(given),))],
    )(*map(in_hbm, given))

    def partial(step, block):
        return kernel_call(
            functools.partial(attend_kernel, (step,), group_rows),
            payload,
            [VMEM] * (1 + len(tables)),
            LIGHT,
            4 * MIB,
        )(block, *tables)

    arrived = [swapped(queries, "seq", step) for step in others]
    partials = [partial(step, block) for step, block in zip(others, arrived)]
    own = partial(0, queries)
    partials = dict(zip(others, partials)) | {0: own}
    kept = kept_steps(seq_count)
    returned = [swapped(partials[step ^ 1], "seq", 1) for step in kept]
    paired = kernel_call(
        functools.partial(pair_kernel, rows),
        pltpu.VMEM((rows * len(kept) + stat_rows(len(kept)), head_dim), jnp.bfloat16),
        [VMEM] * (2 * len(kept)),
        LIGHT,
        4 * MIB,
    )(*[partials[step] for step in kept], *returned)
    gathered = dict(enumerate([paired] + [swapped(paired, "seq", step) for step in others]))
    weights = in_vmem(out_weight)
    lines = drafts * req_dev
    running = ()
    for group in (kept, [step for step in range(seq_count) if step not in kept]):
        finished = kernel_call(
            functools.partial(merge_kernel, group, group, kept, rows_dev, drafts),
            [pltpu.VMEM((rows, head_dim), jnp.bfloat16)] * len(group),
            [VMEM] * len(group),
            LIGHT,
            4 * MIB,
            [pltpu.VMEM((len(group), rows, head_dim), jnp.float32)] * 2,
        )(*[gathered[step] for step in group])
        first = not running
        running = kernel_call(
            functools.partial(project_kernel, group, first),
            [pltpu.VMEM((lines, wide), jnp.float32)]
            if first
            else [pltpu.VMEM((lines // head_count, wide), jnp.bfloat16)] * head_count,
            [VMEM] * (len(group) + 1 + len(running)),
            LIGHT,
            8 * MIB if first else 8 * MIB,
        )(*finished, weights, *running)
    shares = running
    summed = [swapped(shares[step], "head", step) for step in range(head_count - 1, 0, -1)]
    return kernel_call(
        sum_kernel,
        jax.ShapeDtypeStruct((drafts // head_count, req_dev, wide), jnp.bfloat16),
        [VMEM] * head_count,
        LIGHT,
        4 * MIB,
    )(shares[0], *summed)


def passed_along(value, axis, steps):
    count = lax.axis_size(axis)
    pairs = [(source, (source + steps) % count) for source in range(count)]
    return lax.ppermute(value, axis, pairs)


def combine_state(first, second):
    top = jnp.maximum(first[0], second[0])
    early = jnp.exp(first[0] - top)
    later = jnp.exp(second[0] - top)
    return (
        top,
        first[1] * early + second[1] * later,
        first[2] * early[..., None] + second[2] * later[..., None],
    )


def shard_partial(block_q, key_block, key_tok, value_block, value_tok, positions, limits):
    raw = jnp.einsum("rhqd,rhkd->rhqk", block_q, key_block, preferred_element_type=jnp.float32)
    scores = raw * (key_tok[:, :, None, :] * (1.0 / math.sqrt(HD)))
    visible = positions[:, None, None, :] <= limits[:, None, :, None]
    masked = jnp.where(visible, scores, NEG_FLOOR)
    top = jnp.max(masked, axis=3)
    weights = jnp.where(visible, jnp.exp(masked - top[..., None]), 0.0)
    total = jnp.sum(weights, axis=3)
    scaled = (weights * value_tok[:, :, None, :]).astype(jnp.bfloat16)
    acc = jnp.einsum("rhqk,rhkd->rhqd", scaled, value_block, preferred_element_type=jnp.float32)
    return (top, total, acc)


def round_the_ring(
    queries,
    key_codes,
    key_scale,
    value_codes,
    value_scale,
    out_weight,
    ctx_len,
    start_shard,
    draft_depth,
):
    seq_count = lax.axis_size("seq")
    here = lax.axis_index("seq")
    req_dev, rows_dev, head_dim = queries.shape
    kv_rows = key_codes.shape[2]
    group_rows = QHEADS // KVH * DRAFT
    key_tok = jnp.repeat(key_scale, BLK, axis=2)
    value_tok = jnp.repeat(value_scale, BLK, axis=2)
    offsets = jnp.mod(here - start_shard, seq_count)
    positions = offsets[:, None] * kv_rows + jnp.arange(kv_rows, dtype=jnp.int32)[None, :]
    base_limit = ctx_len - DRAFT
    draft_ids = jnp.arange(DRAFT, dtype=jnp.int32)

    def row_limits(first, count):
        draft_of = (first + jnp.arange(count, dtype=jnp.int32)) % DRAFT
        pick = (draft_of[:, None] == draft_ids[None, :]).astype(jnp.int32)
        return base_limit[:, None] + jnp.sum(draft_depth[:, None, :] * pick[None], axis=2)

    def turn(step, carry):
        block_q, top, total, acc = carry
        anchor = jnp.mod(here - step, seq_count)
        first = anchor * rows_dev
        head_pick = first // group_rows
        key_block = lax.dynamic_slice_in_dim(key_codes, head_pick, 1, 1)
        value_block = lax.dynamic_slice_in_dim(value_codes, head_pick, 1, 1)
        key_sel = lax.dynamic_slice_in_dim(key_tok, head_pick, 1, 1)
        value_sel = lax.dynamic_slice_in_dim(value_tok, head_pick, 1, 1)
        part = shard_partial(
            block_q[:, None],
            key_block,
            key_sel,
            value_block,
            value_sel,
            positions,
            row_limits(first, rows_dev),
        )
        merged = combine_state((top, total, acc), (part[0][:, 0], part[1][:, 0], part[2][:, 0]))
        moved = passed_along(
            (block_q.astype(jnp.float32), merged[0], merged[1], merged[2]), "seq", 1
        )
        return (moved[0].astype(jnp.bfloat16), moved[1], moved[2], moved[3])

    start_state = (
        queries,
        jnp.full((req_dev, rows_dev), NEG_FLOOR, jnp.float32),
        jnp.zeros((req_dev, rows_dev), jnp.float32),
        jnp.zeros((req_dev, rows_dev, head_dim), jnp.float32),
    )
    final = lax.fori_loop(0, seq_count, turn, start_state)
    attention = (final[3] / final[2][..., None]).astype(jnp.bfloat16)
    gathered = lax.all_gather(attention, "seq", axis=1, tiled=True)
    heads = gathered.shape[1] // DRAFT
    arranged = gathered.reshape(req_dev, heads, DRAFT, head_dim)
    width_dev = out_weight.shape[1]
    flat = jnp.transpose(arranged, (2, 0, 1, 3)).reshape(DRAFT * req_dev, heads * head_dim)
    result = jnp.dot(flat, out_weight, preferred_element_type=jnp.float32)
    summed = lax.psum_scatter(
        result.reshape(DRAFT, req_dev, width_dev), "head", scatter_dimension=0, tiled=True
    )
    return summed.astype(jnp.bfloat16)


def on_device(*arrays):
    queries, key_codes = arrays[:2]
    seq_count, head_count = lax.axis_size("seq"), lax.axis_size("head")
    req_dev, rows_dev, head_dim = queries.shape
    paired = all(count & (count - 1) == 0 for count in (seq_count, head_count))
    tiled = req_dev * rows_dev == head_dim and rows_dev % (2 * DRAFT) == 0
    whole = seq_count * rows_dev // key_codes.shape[1] % rows_dev == 0
    if paired and tiled and whole and DRAFT % head_count == 0:
        return with_kernels(*arrays)
    return round_the_ring(*arrays)


def solution(mesh):
    placed = (
        P("req", ("head", "seq"), None),
        P("req", "head", "seq", None),
        P("req", "head", "seq"),
        P("req", "head", "seq", None),
        P("req", "head", "seq"),
        P("head", "seq"),
        P("req"),
        P("req"),
        P("req", None),
    )
    return jax.shard_map(
        on_device, mesh=mesh, in_specs=placed, out_specs=P("head", "req", "seq"), check_vma=False
    )
```

```python
import functools
import math

import jax
import jax.numpy as jnp
from jax import lax
from jax.experimental import pallas as pl
from jax.experimental.pallas import tpu as pltpu
from jax.sharding import PartitionSpec as P

QHEADS = 128
KVH = 8
HD = 128
DRAFT = 4
BLK = 64

NEG_FLOOR = -1e30
STAT_ROWS = 16
MIB = 1 << 20
HEAVY = 20_000_000_000
LIGHT = 4_000_000_000
VMEM = pl.BlockSpec(memory_space=pltpu.VMEM)


def swapped(value, axis, step):
    count = lax.axis_size(axis)
    return lax.ppermute(value, axis, [(source, source ^ step) for source in range(count)])


def in_vmem(value):
    return pltpu.with_memory_space_constraint(value, pltpu.VMEM)


def in_hbm(value):
    return pltpu.with_memory_space_constraint(value, pltpu.HBM)


def kernel_call(kernel, out_shape, in_specs, flops, limit, scratch=(), aliases=None):
    return pl.pallas_call(
        kernel,
        out_shape=out_shape,
        in_specs=in_specs,
        out_specs=jax.tree.map(lambda _: VMEM, out_shape),
        scratch_shapes=list(scratch),
        input_output_aliases=aliases or {},
        cost_estimate=pl.CostEstimate(flops=flops, bytes_accessed=0, transcendentals=0),
        compiler_params=pltpu.CompilerParams(vmem_limit_bytes=limit),
    )


def three_parts(value):
    high = value.astype(jnp.bfloat16).astype(jnp.float32)
    rest = value - high
    middle = rest.astype(jnp.bfloat16).astype(jnp.float32)
    return (high, middle, rest - middle)


def attend(step, group_rows, q_ref, key_ref, value_ref, key_table, value_table, bias_ref, out_ref):
    req_dev, rows_dev, head_dim = q_ref.shape
    head = (lax.axis_index("seq") ^ step) * rows_dev // group_rows
    heads = key_ref.shape[1]
    reqs = range(req_dev)
    raw = [
        lax.dot_general(
            q_ref[req],
            key_ref[req, head],
            (((1,), (1,)), ((), ())),
            preferred_element_type=jnp.float32,
        )
        for req in reqs
    ]
    copies = rows_dev // bias_ref.shape[1]
    masked = [
        raw[req] * key_table[pl.ds(req * heads + head, 1), :]
        + jnp.concatenate([bias_ref[req]] * copies, axis=0)
        for req in reqs
    ]
    top = [jnp.max(part, axis=1, keepdims=True) for part in masked]
    weights = [jnp.exp2(part - high) for part, high in zip(masked, top)]
    total = [
        jnp.where(high > 0.5 * NEG_FLOOR, jnp.sum(part, axis=1, keepdims=True), 0.0)
        for part, high in zip(weights, top)
    ]
    scaled = [
        (weights[req] * value_table[pl.ds(req * heads + head, 1), :]).astype(jnp.bfloat16)
        for req in reqs
    ]
    acc = [
        jnp.dot(scaled[req], value_ref[req, head], preferred_element_type=jnp.float32)
        for req in reqs
    ]
    rows = req_dev * rows_dev
    stat_lane = lax.broadcasted_iota(jnp.int32, (rows, head_dim), 1)
    stats = jnp.zeros((rows, head_dim), jnp.float32)
    pieces = three_parts(jnp.concatenate(top, axis=0)) + three_parts(jnp.concatenate(total, axis=0))
    for at, part in enumerate(pieces):
        stats = jnp.where(stat_lane == at, part, stats)
    out_ref[:rows, :] = jnp.concatenate(acc, axis=0).astype(jnp.bfloat16)
    out_ref[rows:, :] = jnp.transpose(stats)[:STAT_ROWS].astype(jnp.bfloat16)


def prepare_kernel(head_dim, *refs):
    given, refs = refs[:8], refs[8:]
    key_ref, value_ref, key_table, value_table, bias_ref, q_ref = refs[:6]
    ctx, start, depth, key_scale, value_scale, sems = refs[6:]
    targets = (ctx, start, depth, key_scale, value_scale, key_ref, value_ref, q_ref)
    copies = [
        pltpu.make_async_copy(source, target, sems.at[at])
        for at, (source, target) in enumerate(zip(given, targets))
    ]
    for copy in copies:
        copy.start()
    req_dev, heads, kv_rows = key_ref.shape[:3]
    blocks = key_scale.shape[2]
    width = kv_rows // blocks
    drafts = depth.shape[1]
    seq_count = lax.axis_size("seq")
    here = lax.axis_index("seq")
    lane = lax.broadcasted_iota(jnp.int32, (1, kv_rows), 1)
    tall = bias_ref.shape[1]
    draft_of = lax.broadcasted_iota(jnp.int32, (tall, kv_rows), 0) % drafts
    for copy in copies[:5]:
        copy.wait()
    factor = math.log2(math.e) / math.sqrt(head_dim)
    for req in range(req_dev):
        for head in range(heads):
            for scale, table, by in ((key_scale, key_table, factor), (value_scale, value_table, 1.0)):
                found = jnp.full((1, kv_rows), scale[req, head, 0] * by, jnp.float32)
                for block in range(1, blocks):
                    found = jnp.where(lane >= block * width, scale[req, head, block] * by, found)
                table[req * heads + head : req * heads + head + 1, :] = found
        first = jnp.where(here >= start[req], here - start[req], here - start[req] + seq_count)
        limit = jnp.full((tall, kv_rows), depth[req, 0], jnp.int32)
        for draft in range(1, drafts):
            limit = jnp.where(draft_of == draft, depth[req, draft], limit)
        limit = limit + (ctx[req] - drafts - first * kv_rows)
        bias_ref[req] = jnp.where(lane <= limit, 0.0, NEG_FLOOR)
    for copy in copies[5:]:
        copy.wait()


def attend_kernel(steps, group_rows, *refs):
    count = len(steps)
    for step, q_ref, out_ref in zip(steps, refs[:count], refs[count + 5 :]):
        attend(step, group_rows, q_ref, *refs[count : count + 5], out_ref)


def kept_steps(count):
    return [step for step in range(count) if step.bit_count() % 2 == 0]


def stat_rows(count):
    return -(-6 * count // STAT_ROWS) * STAT_ROWS


def read_stats(ref, first):
    stats = ref[first:, :].astype(jnp.float32)
    return [
        (
            stats[at : at + 1] + stats[at + 1 : at + 2] + stats[at + 2 : at + 3],
            stats[at + 3 : at + 4] + stats[at + 4 : at + 5] + stats[at + 5 : at + 6],
        )
        for at in range(0, stats.shape[0] - 5, 6)
    ]


def combine_stats(stats):
    top = functools.reduce(jnp.maximum, [part[0] for part in stats])
    factors = [jnp.exp2(part[0] - top) for part in stats]
    total = sum(part[1] * factor for part, factor in zip(stats, factors))
    return top, total, factors


def as_columns(rows):
    lanes = rows[0].shape[1]
    which = lax.broadcasted_iota(jnp.int32, (lanes, lanes), 0)
    table = jnp.zeros((lanes, lanes), jnp.float32)
    for at, row in enumerate(rows):
        table = jnp.where(which == at, row, table)
    turned = jnp.transpose(table)
    return [turned[:, at : at + 1] for at in range(len(rows))]


def pair_kernel(rows, *refs):
    kept = (len(refs) - 1) // 2
    pairs = list(zip(refs[:kept], refs[kept : 2 * kept]))
    out_ref = refs[-1]
    found, columns = [], []
    for pair in pairs:
        top, total, factors = combine_stats([read_stats(ref, rows)[0] for ref in pair])
        found += [*three_parts(top), *three_parts(total)]
        columns += factors
    columns = as_columns(columns)
    merged = [
        sum(
            ref[:rows, :].astype(jnp.float32) * columns[2 * at + side]
            for side, ref in enumerate(pair)
        )
        for at, pair in enumerate(pairs)
    ]
    spare = out_ref.shape[0] - rows * kept - len(found)
    found.append(jnp.zeros((spare, out_ref.shape[1]), jnp.float32))
    for at, part in enumerate(merged):
        out_ref[at * rows : (at + 1) * rows, :] = part.astype(jnp.bfloat16)
    out_ref[rows * kept :, :] = jnp.concatenate(found, axis=0).astype(jnp.bfloat16)


def merge_kernel(peers, blocks, kept, rows_dev, drafts, *refs):
    count = len(peers)
    part_refs, out_refs = refs[:count], refs[count : count + len(blocks)]
    held, ordered = refs[count + len(blocks) :]
    rows = held.shape[1]
    req_dev = rows // rows_dev
    heads = rows_dev // drafts
    share = drafts // lax.axis_size("head")
    mine = lax.axis_index("head")
    stats = [read_stats(ref, rows * len(kept)) for ref in part_refs]
    places = [[kept.index(block ^ peer) for peer in peers] for block in blocks]
    table = []
    for place in places:
        _, total, factors = combine_stats([stat[at] for stat, at in zip(stats, place)])
        table += [factor / total for factor in factors]
    columns = iter(as_columns(table))
    for block, place in enumerate(places):
        held[block] = sum(
            ref[at * rows : (at + 1) * rows, :].astype(jnp.float32) * next(columns)
            for ref, at in zip(part_refs, place)
        )
    for block in range(len(blocks)):
        for req in range(req_dev):
            for draft in range(drafts):
                taken = held[block, pl.ds(req * rows_dev + draft, heads, stride=drafts), :]
                place = (draft // share) ^ mine
                row = (place * share + draft % share) * req_dev + req
                ordered[block, pl.ds(row, heads, stride=drafts * req_dev), :] = taken
    for block in range(len(blocks)):
        out_refs[block][...] = ordered[block].astype(jnp.bfloat16)


def project_parts(ref, depth):
    head_dim = ref.shape[1]
    heads = depth // head_dim
    lines = ref.shape[0] // heads
    return jnp.concatenate(
        [ref[head * lines : (head + 1) * lines, :] for head in range(heads)], axis=1
    )


def project_kernel(steps, first, *refs):
    count = len(steps)
    x_refs = refs[:count]
    weight_ref = refs[count]
    before = None if first else refs[count + 1]
    out_refs = refs[count + 1 if first else count + 2 :]
    here = lax.axis_index("seq")
    depth = weight_ref.shape[0] // lax.axis_size("seq")
    x_parts = [project_parts(ref, depth) for ref in x_refs]
    wide = weight_ref.shape[1]
    cut = min(wide, 512)
    tall = out_refs[0].shape[0]
    for column in range(0, wide, cut):
        spot = slice(column, column + cut)
        found = None if first else before[:, spot]
        for step, part in zip(steps, x_parts):
            start = pl.multiple_of((here ^ step) * depth, depth)
            product = jnp.dot(
                part, weight_ref[pl.ds(start, depth), spot], preferred_element_type=jnp.float32
            )
            found = product if found is None else found + product
        for piece, out_ref in enumerate(out_refs):
            out_ref[:, spot] = found[piece * tall : (piece + 1) * tall].astype(out_ref.dtype)


def sum_kernel(*refs):
    out_ref = refs[-1]
    total = refs[0][...].astype(jnp.float32)
    for ref in refs[1:-1]:
        total = total + ref[...].astype(jnp.float32)
    out_ref[...] = total.astype(out_ref.dtype).reshape(out_ref.shape)


def with_kernels(
    queries,
    key_codes,
    key_scale,
    value_codes,
    value_scale,
    out_weight,
    ctx_len,
    start_shard,
    draft_depth,
):
    seq_count = lax.axis_size("seq")
    head_count = lax.axis_size("head")
    req_dev, rows_dev, head_dim = queries.shape
    group_rows = seq_count * rows_dev // key_codes.shape[1]
    drafts = draft_depth.shape[1]
    rows = req_dev * rows_dev
    wide = out_weight.shape[1]
    others = range(1, seq_count)
    kv_heads, kv_rows = key_codes.shape[1:3]
    tall = 2 * drafts
    payload = pltpu.VMEM((rows + STAT_ROWS, head_dim), jnp.bfloat16)
    given = (
        ctx_len,
        start_shard,
        draft_depth,
        key_scale,
        value_scale,
        key_codes,
        value_codes,
        queries,
    )
    *tables, own_queries = kernel_call(
        functools.partial(prepare_kernel, head_dim),
        [
            pltpu.VMEM(key_codes.shape, key_codes.dtype),
            pltpu.VMEM(value_codes.shape, value_codes.dtype),
            pltpu.VMEM((req_dev * kv_heads, kv_rows), jnp.float32),
            pltpu.VMEM((req_dev * kv_heads, kv_rows), jnp.float32),
            pltpu.VMEM((req_dev, tall, kv_rows), jnp.float32),
            pltpu.VMEM(queries.shape, queries.dtype),
        ],
        [pl.BlockSpec(memory_space=pltpu.HBM)] * len(given),
        1000000,
        8 * MIB,
        [pltpu.SMEM(part.shape, part.dtype) for part in given[:5]]
        + [pltpu.SemaphoreType.DMA((len(given),))],
    )(*map(in_hbm, given))

    def partial(step, block):
        return kernel_call(
            functools.partial(attend_kernel, (step,), group_rows),
            payload,
            [VMEM] * (1 + len(tables)),
            {0: 20000000000, 1: 100000, 2: 1000000, 3: 100000}[step],
            4 * MIB,
        )(block, *tables)

    arrived = [swapped(queries, "seq", step) for step in others]
    partials = [partial(step, block) for step, block in zip(others, arrived)]
    own = partial(0, own_queries)
    partials = dict(zip(others, partials)) | {0: own}
    kept = kept_steps(seq_count)
    returned = [swapped(partials[step ^ 1], "seq", 1) for step in kept]
    paired = kernel_call(
        functools.partial(pair_kernel, rows),
        pltpu.VMEM((rows * len(kept) + stat_rows(len(kept)), head_dim), jnp.bfloat16),
        [VMEM] * (2 * len(kept)),
        1000000,
        4 * MIB,
    )(*[partials[step] for step in kept], *returned)
    gathered = dict(enumerate([paired] + [swapped(paired, "seq", step) for step in others]))
    weights = in_vmem(out_weight)
    lines = drafts * req_dev
    running = ()
    for group in (kept, [step for step in range(seq_count) if step not in kept]):
        finished = kernel_call(
            functools.partial(merge_kernel, group, group, kept, rows_dev, drafts),
            [pltpu.VMEM((rows, head_dim), jnp.bfloat16)] * len(group),
            [VMEM] * len(group),
            1000000,
            4 * MIB,
            [pltpu.VMEM((len(group), rows, head_dim), jnp.float32)] * 2,
        )(*[gathered[step] for step in group])
        first = not running
        running = kernel_call(
            functools.partial(project_kernel, group, first),
            [pltpu.VMEM((lines, wide), jnp.float32)]
            if first
            else [pltpu.VMEM((lines // head_count, wide), jnp.bfloat16)] * head_count,
            [VMEM] * (len(group) + 1 + len(running)),
            1000000,
            8 * MIB if first else 8 * MIB,
        )(*finished, weights, *running)
    shares = running
    summed = [swapped(shares[step], "head", step) for step in range(head_count - 1, 0, -1)]
    return kernel_call(
        sum_kernel,
        jax.ShapeDtypeStruct((drafts // head_count, req_dev, wide), jnp.bfloat16),
        [VMEM] * head_count,
        LIGHT,
        4 * MIB,
    )(shares[0], *summed)


def passed_along(value, axis, steps):
    count = lax.axis_size(axis)
    pairs = [(source, (source + steps) % count) for source in range(count)]
    return lax.ppermute(value, axis, pairs)


def combine_state(first, second):
    top = jnp.maximum(first[0], second[0])
    early = jnp.exp(first[0] - top)
    later = jnp.exp(second[0] - top)
    return (
        top,
        first[1] * early + second[1] * later,
        first[2] * early[..., None] + second[2] * later[..., None],
    )


def shard_partial(block_q, key_block, key_tok, value_block, value_tok, positions, limits):
    raw = jnp.einsum("rhqd,rhkd->rhqk", block_q, key_block, preferred_element_type=jnp.float32)
    scores = raw * (key_tok[:, :, None, :] * (1.0 / math.sqrt(HD)))
    visible = positions[:, None, None, :] <= limits[:, None, :, None]
    masked = jnp.where(visible, scores, NEG_FLOOR)
    top = jnp.max(masked, axis=3)
    weights = jnp.where(visible, jnp.exp(masked - top[..., None]), 0.0)
    total = jnp.sum(weights, axis=3)
    scaled = (weights * value_tok[:, :, None, :]).astype(jnp.bfloat16)
    acc = jnp.einsum("rhqk,rhkd->rhqd", scaled, value_block, preferred_element_type=jnp.float32)
    return (top, total, acc)


def round_the_ring(
    queries,
    key_codes,
    key_scale,
    value_codes,
    value_scale,
    out_weight,
    ctx_len,
    start_shard,
    draft_depth,
):
    seq_count = lax.axis_size("seq")
    here = lax.axis_index("seq")
    req_dev, rows_dev, head_dim = queries.shape
    kv_rows = key_codes.shape[2]
    group_rows = QHEADS // KVH * DRAFT
    key_tok = jnp.repeat(key_scale, BLK, axis=2)
    value_tok = jnp.repeat(value_scale, BLK, axis=2)
    offsets = jnp.mod(here - start_shard, seq_count)
    positions = offsets[:, None] * kv_rows + jnp.arange(kv_rows, dtype=jnp.int32)[None, :]
    base_limit = ctx_len - DRAFT
    draft_ids = jnp.arange(DRAFT, dtype=jnp.int32)

    def row_limits(first, count):
        draft_of = (first + jnp.arange(count, dtype=jnp.int32)) % DRAFT
        pick = (draft_of[:, None] == draft_ids[None, :]).astype(jnp.int32)
        return base_limit[:, None] + jnp.sum(draft_depth[:, None, :] * pick[None], axis=2)

    def turn(step, carry):
        block_q, top, total, acc = carry
        anchor = jnp.mod(here - step, seq_count)
        first = anchor * rows_dev
        head_pick = first // group_rows
        key_block = lax.dynamic_slice_in_dim(key_codes, head_pick, 1, 1)
        value_block = lax.dynamic_slice_in_dim(value_codes, head_pick, 1, 1)
        key_sel = lax.dynamic_slice_in_dim(key_tok, head_pick, 1, 1)
        value_sel = lax.dynamic_slice_in_dim(value_tok, head_pick, 1, 1)
        part = shard_partial(
            block_q[:, None],
            key_block,
            key_sel,
            value_block,
            value_sel,
            positions,
            row_limits(first, rows_dev),
        )
        merged = combine_state((top, total, acc), (part[0][:, 0], part[1][:, 0], part[2][:, 0]))
        moved = passed_along(
            (block_q.astype(jnp.float32), merged[0], merged[1], merged[2]), "seq", 1
        )
        return (moved[0].astype(jnp.bfloat16), moved[1], moved[2], moved[3])

    start_state = (
        queries,
        jnp.full((req_dev, rows_dev), NEG_FLOOR, jnp.float32),
        jnp.zeros((req_dev, rows_dev), jnp.float32),
        jnp.zeros((req_dev, rows_dev, head_dim), jnp.float32),
    )
    final = lax.fori_loop(0, seq_count, turn, start_state)
    attention = (final[3] / final[2][..., None]).astype(jnp.bfloat16)
    gathered = lax.all_gather(attention, "seq", axis=1, tiled=True)
    heads = gathered.shape[1] // DRAFT
    arranged = gathered.reshape(req_dev, heads, DRAFT, head_dim)
    width_dev = out_weight.shape[1]
    flat = jnp.transpose(arranged, (2, 0, 1, 3)).reshape(DRAFT * req_dev, heads * head_dim)
    result = jnp.dot(flat, out_weight, preferred_element_type=jnp.float32)
    summed = lax.psum_scatter(
        result.reshape(DRAFT, req_dev, width_dev), "head", scatter_dimension=0, tiled=True
    )
    return summed.astype(jnp.bfloat16)


def on_device(*arrays):
    queries, key_codes = arrays[:2]
    seq_count, head_count = lax.axis_size("seq"), lax.axis_size("head")
    req_dev, rows_dev, head_dim = queries.shape
    paired = all(count & (count - 1) == 0 for count in (seq_count, head_count))
    tiled = req_dev * rows_dev == head_dim and rows_dev % (2 * DRAFT) == 0
    whole = seq_count * rows_dev // key_codes.shape[1] % rows_dev == 0
    if paired and tiled and whole and DRAFT % head_count == 0:
        return with_kernels(*arrays)
    return round_the_ring(*arrays)


def solution(mesh):
    placed = (
        P("req", ("head", "seq"), None),
        P("req", "head", "seq", None),
        P("req", "head", "seq"),
        P("req", "head", "seq", None),
        P("req", "head", "seq"),
        P("head", "seq"),
        P("req"),
        P("req"),
        P("req", None),
    )
    return jax.shard_map(
        on_device, mesh=mesh, in_specs=placed, out_specs=P("head", "req", "seq"), check_vma=False
    )
```

```python
import functools
import math

import jax
import jax.numpy as jnp
from jax import lax
from jax.experimental import pallas as pl
from jax.experimental.pallas import tpu as pltpu
from jax.sharding import PartitionSpec as P

QHEADS = 128
KVH = 8
HD = 128
DRAFT = 4
BLK = 64

NEG_FLOOR = -1e30
STAT_ROWS = 16
MIB = 1 << 20
LONG = 20_000_000_000
SHORT = 1_000_000
GRANT = 8 * MIB
LATER_GRANT = GRANT + 136 * 1024
VMEM = pl.BlockSpec(memory_space=pltpu.VMEM)


def swapped(value, axis, step):
    count = lax.axis_size(axis)
    return lax.ppermute(value, axis, [(source, source ^ step) for source in range(count)])


def in_vmem(value):
    return pltpu.with_memory_space_constraint(value, pltpu.VMEM)


def in_hbm(value):
    return pltpu.with_memory_space_constraint(value, pltpu.HBM)


def kernel_call(kernel, out_shape, in_specs, flops, limit, scratch=()):
    return pl.pallas_call(
        kernel,
        out_shape=out_shape,
        in_specs=in_specs,
        out_specs=jax.tree.map(lambda _: VMEM, out_shape),
        scratch_shapes=list(scratch),
        cost_estimate=pl.CostEstimate(flops=flops, bytes_accessed=0, transcendentals=0),
        compiler_params=pltpu.CompilerParams(vmem_limit_bytes=limit),
    )


def three_parts(value):
    high = value.astype(jnp.bfloat16).astype(jnp.float32)
    rest = value - high
    middle = rest.astype(jnp.bfloat16).astype(jnp.float32)
    return (high, middle, rest - middle)


def attend(step, group_rows, q_ref, key_ref, value_ref, key_table, value_table, bias_ref, out_ref):
    req_dev, rows_dev, head_dim = q_ref.shape
    head = (lax.axis_index("seq") ^ step) * rows_dev // group_rows
    heads = key_ref.shape[1]
    reqs = range(req_dev)
    raw = [
        lax.dot_general(
            q_ref[req],
            key_ref[req, head],
            (((1,), (1,)), ((), ())),
            preferred_element_type=jnp.float32,
        )
        for req in reqs
    ]
    copies = rows_dev // bias_ref.shape[1]
    masked = [
        raw[req] * key_table[pl.ds(req * heads + head, 1), :]
        + jnp.concatenate([bias_ref[req]] * copies, axis=0)
        for req in reqs
    ]
    top = [jnp.max(part, axis=1, keepdims=True) for part in masked]
    weights = [jnp.exp2(part - high) for part, high in zip(masked, top)]
    total = [
        jnp.where(high > 0.5 * NEG_FLOOR, jnp.sum(part, axis=1, keepdims=True), 0.0)
        for part, high in zip(weights, top)
    ]
    scaled = [
        (weights[req] * value_table[pl.ds(req * heads + head, 1), :]).astype(jnp.bfloat16)
        for req in reqs
    ]
    acc = [
        jnp.dot(scaled[req], value_ref[req, head], preferred_element_type=jnp.float32)
        for req in reqs
    ]
    rows = req_dev * rows_dev
    stat_lane = lax.broadcasted_iota(jnp.int32, (rows, head_dim), 1)
    stats = jnp.zeros((rows, head_dim), jnp.float32)
    pieces = three_parts(jnp.concatenate(top, axis=0)) + three_parts(jnp.concatenate(total, axis=0))
    for at, part in enumerate(pieces):
        stats = jnp.where(stat_lane == at, part, stats)
    out_ref[:rows, :] = jnp.concatenate(acc, axis=0).astype(jnp.bfloat16)
    out_ref[rows:, :] = jnp.transpose(stats)[:STAT_ROWS].astype(jnp.bfloat16)


def prepare_kernel(head_dim, *refs):
    given, refs = refs[:8], refs[8:]
    key_ref, value_ref, key_table, value_table, bias_ref, q_ref = refs[:6]
    ctx, start, depth, key_scale, value_scale, sems = refs[6:]
    targets = (ctx, start, depth, key_scale, value_scale, key_ref, value_ref, q_ref)
    copies = [
        pltpu.make_async_copy(source, target, sems.at[at])
        for at, (source, target) in enumerate(zip(given, targets))
    ]
    for copy in copies:
        copy.start()
    req_dev, heads, kv_rows = key_ref.shape[:3]
    blocks = key_scale.shape[2]
    width = kv_rows // blocks
    drafts = depth.shape[1]
    seq_count = lax.axis_size("seq")
    here = lax.axis_index("seq")
    lane = lax.broadcasted_iota(jnp.int32, (1, kv_rows), 1)
    tall = bias_ref.shape[1]
    draft_of = lax.broadcasted_iota(jnp.int32, (tall, kv_rows), 0) % drafts
    for copy in copies[:5]:
        copy.wait()
    factor = math.log2(math.e) / math.sqrt(head_dim)
    for scale, table, by in ((key_scale, key_table, factor), (value_scale, value_table, 1.0)):
        scales = jnp.concatenate([scale[req] for req in range(req_dev)], axis=0) * by
        found = jnp.broadcast_to(scales[:, :1], table.shape)
        for block in range(1, blocks):
            found = jnp.where(lane >= block * width, scales[:, block : block + 1], found)
        table[...] = found
    for req in range(req_dev):
        first = jnp.where(here >= start[req], here - start[req], here - start[req] + seq_count)
        limit = jnp.full((tall, kv_rows), depth[req, 0], jnp.int32)
        for draft in range(1, drafts):
            limit = jnp.where(draft_of == draft, depth[req, draft], limit)
        limit = limit + (ctx[req] - drafts - first * kv_rows)
        bias_ref[req] = jnp.where(lane <= limit, 0.0, NEG_FLOOR)
    for copy in copies[5:]:
        copy.wait()


def attend_kernel(steps, group_rows, *refs):
    count = len(steps)
    out_ref = refs[-1]
    tall = out_ref.shape[0] // count
    for at, (step, q_ref) in enumerate(zip(steps, refs[:count])):
        spot = out_ref.at[at * tall : (at + 1) * tall]
        attend(step, group_rows, q_ref, *refs[count : count + 5], spot)


def kept_steps(count):
    return [step for step in range(count) if step % 2 == 0]


def stat_rows(count):
    return -(-6 * count // STAT_ROWS) * STAT_ROWS


def read_stats(ref, first):
    stats = ref[first:, :].astype(jnp.float32)
    return [
        (
            stats[at : at + 1] + stats[at + 1 : at + 2] + stats[at + 2 : at + 3],
            stats[at + 3 : at + 4] + stats[at + 4 : at + 5] + stats[at + 5 : at + 6],
        )
        for at in range(0, stats.shape[0] - 5, 6)
    ]


def combine_stats(stats):
    top = functools.reduce(jnp.maximum, [part[0] for part in stats])
    factors = [jnp.exp2(part[0] - top) for part in stats]
    total = sum(part[1] * factor for part, factor in zip(stats, factors))
    return top, total, factors


def as_columns(rows):
    lanes = rows[0].shape[1]
    which = lax.broadcasted_iota(jnp.int32, (lanes, lanes), 0)
    table = jnp.zeros((lanes, lanes), jnp.float32)
    for at, row in enumerate(rows):
        table = jnp.where(which == at, row, table)
    turned = jnp.transpose(table)
    return [turned[:, at : at + 1] for at in range(len(rows))]


def pair_kernel(rows, kept, *refs):
    tall = refs[0].shape[0] // kept
    pairs = [
        [ref.at[at * tall : (at + 1) * tall] for ref in refs[:2]] for at in range(kept)
    ]
    out_ref = refs[-1]
    found, columns = [], []
    for pair in pairs:
        top, total, factors = combine_stats([read_stats(ref, rows)[0] for ref in pair])
        found += [*three_parts(top), *three_parts(total)]
        columns += factors
    columns = as_columns(columns)
    merged = [
        sum(
            ref[:rows, :].astype(jnp.float32) * columns[2 * at + side]
            for side, ref in enumerate(pair)
        )
        for at, pair in enumerate(pairs)
    ]
    spare = out_ref.shape[0] - rows * kept - len(found)
    found.append(jnp.zeros((spare, out_ref.shape[1]), jnp.float32))
    for at, part in enumerate(merged):
        out_ref[at * rows : (at + 1) * rows, :] = part.astype(jnp.bfloat16)
    out_ref[rows * kept :, :] = jnp.concatenate(found, axis=0).astype(jnp.bfloat16)


def merged_blocks(group, kept, rows_dev, drafts, part_refs, held, ordered):
    rows = (part_refs[0].shape[0] - stat_rows(len(kept))) // len(kept)
    req_dev = rows // rows_dev
    heads = rows_dev // drafts
    lines = drafts * req_dev
    share = drafts // lax.axis_size("head")
    mine = lax.axis_index("head")
    stats = [read_stats(ref, rows * len(kept)) for ref in part_refs]
    places = [[kept.index(block ^ peer) for peer in group] for block in group]
    table = []
    for place in places:
        _, total, factors = combine_stats([stat[at] for stat, at in zip(stats, place)])
        table += [factor / total for factor in factors]
    columns = iter(as_columns(table))
    for block, place in enumerate(places):
        held[block, :rows, :] = sum(
            ref[at * rows : (at + 1) * rows, :].astype(jnp.float32) * next(columns)
            for ref, at in zip(part_refs, place)
        )
    for block in range(len(group)):
        for req in range(req_dev):
            for draft in range(drafts):
                taken = held[block, pl.ds(req * rows_dev + draft, heads, stride=drafts), :]
                place = (draft // share) ^ mine
                row = (place * share + draft % share) * req_dev + req
                ordered[block, pl.ds(row, heads, stride=lines), :] = taken
    return [
        jnp.concatenate(
            [ordered[block, head * lines : (head + 1) * lines, :] for head in range(heads)], axis=1
        ).astype(jnp.bfloat16)
        for block in range(len(group))
    ]


def project_kernel(group, kept, rows_dev, drafts, first, *refs):
    count = len(group)
    part_refs, weight_ref = refs[:count], refs[count]
    before = None if first else refs[count + 1]
    out_refs = refs[count + 1 if first else count + 2 : -2]
    parts = merged_blocks(group, kept, rows_dev, drafts, part_refs, *refs[-2:])
    here = lax.axis_index("seq")
    depth = weight_ref.shape[0] // lax.axis_size("seq")
    wide = weight_ref.shape[1]
    cut = min(wide, 512)
    tall = out_refs[0].shape[0]
    for column in range(0, wide, cut):
        spot = slice(column, column + cut)
        found = None if first else before[:, spot]
        for step, part in zip(group, parts):
            start = pl.multiple_of((here ^ step) * depth, depth)
            product = jnp.dot(
                part, weight_ref[pl.ds(start, depth), spot], preferred_element_type=jnp.float32
            )
            found = product if found is None else found + product
        for piece, out_ref in enumerate(out_refs):
            out_ref[:, spot] = found[piece * tall : (piece + 1) * tall].astype(out_ref.dtype)


def sum_kernel(*refs):
    out_ref = refs[-1]
    total = refs[0][...].astype(jnp.float32)
    for ref in refs[1:-1]:
        total = total + ref[...].astype(jnp.float32)
    out_ref[...] = total.astype(out_ref.dtype).reshape(out_ref.shape)


def with_kernels(
    queries,
    key_codes,
    key_scale,
    value_codes,
    value_scale,
    out_weight,
    ctx_len,
    start_shard,
    draft_depth,
):
    seq_count = lax.axis_size("seq")
    head_count = lax.axis_size("head")
    req_dev, rows_dev, head_dim = queries.shape
    group_rows = seq_count * rows_dev // key_codes.shape[1]
    drafts = draft_depth.shape[1]
    rows = req_dev * rows_dev
    wide = out_weight.shape[1]
    others = range(1, seq_count)
    kv_heads, kv_rows = key_codes.shape[1:3]
    tall = 2 * drafts
    given = (
        ctx_len,
        start_shard,
        draft_depth,
        key_scale,
        value_scale,
        key_codes,
        value_codes,
        queries,
    )
    *tables, own_queries = kernel_call(
        functools.partial(prepare_kernel, head_dim),
        [
            pltpu.VMEM(key_codes.shape, key_codes.dtype),
            pltpu.VMEM(value_codes.shape, value_codes.dtype),
            pltpu.VMEM((req_dev * kv_heads, kv_rows), jnp.float32),
            pltpu.VMEM((req_dev * kv_heads, kv_rows), jnp.float32),
            pltpu.VMEM((req_dev, tall, kv_rows), jnp.float32),
            pltpu.VMEM(queries.shape, queries.dtype),
        ],
        [pl.BlockSpec(memory_space=pltpu.HBM)] * len(given),
        SHORT,
        8 * MIB,
        [pltpu.SMEM(part.shape, part.dtype) for part in given[:3]]
        + [pltpu.VMEM(part.shape, part.dtype) for part in given[3:5]]
        + [pltpu.SemaphoreType.DMA((len(given),))],
    )(*map(in_hbm, given))

    def partial(steps, flops):
        return kernel_call(
            functools.partial(attend_kernel, steps, group_rows),
            pltpu.VMEM((len(steps) * (rows + STAT_ROWS), head_dim), jnp.bfloat16),
            [VMEM] * (len(steps) + len(tables)),
            flops,
            4 * MIB,
        )(*[blocks[step] for step in steps], *tables)

    blocks = {step: swapped(queries, "seq", step) for step in others} | {0: own_queries}
    kept = kept_steps(seq_count)
    handed = partial([step ^ 1 for step in kept], LONG)
    returned = swapped(handed, "seq", 1)
    mine = partial(kept, LONG)
    paired = kernel_call(
        functools.partial(pair_kernel, rows, len(kept)),
        pltpu.VMEM((rows * len(kept) + stat_rows(len(kept)), head_dim), jnp.bfloat16),
        [VMEM] * 2,
        SHORT,
        4 * MIB,
    )(mine, returned)
    gathered = dict(enumerate([paired] + [swapped(paired, "seq", step) for step in others]))
    weights = in_vmem(out_weight)
    lines = drafts * req_dev
    running = ()
    for group in (kept, [step for step in range(seq_count) if step not in kept]):
        first = not running
        running = kernel_call(
            functools.partial(project_kernel, group, kept, rows_dev, drafts, first),
            [pltpu.VMEM((lines, wide), jnp.float32)]
            if first
            else [pltpu.VMEM((lines // head_count, wide), jnp.bfloat16)] * head_count,
            [VMEM] * (len(group) + 1 + len(running)),
            SHORT,
            GRANT if first else LATER_GRANT,
            [pltpu.VMEM((len(group), rows + lines, head_dim), jnp.float32)] * 2,
        )(*[gathered[step] for step in group], weights, *running)
    shares = running
    summed = [swapped(shares[step], "head", step) for step in range(head_count - 1, 0, -1)]
    return kernel_call(
        sum_kernel,
        jax.ShapeDtypeStruct((drafts // head_count, req_dev, wide), jnp.bfloat16),
        [VMEM] * head_count,
        SHORT,
        4 * MIB,
    )(shares[0], *summed)


def passed_along(value, axis, steps):
    count = lax.axis_size(axis)
    pairs = [(source, (source + steps) % count) for source in range(count)]
    return lax.ppermute(value, axis, pairs)


def combine_state(first, second):
    top = jnp.maximum(first[0], second[0])
    early = jnp.exp(first[0] - top)
    later = jnp.exp(second[0] - top)
    return (
        top,
        first[1] * early + second[1] * later,
        first[2] * early[..., None] + second[2] * later[..., None],
    )


def shard_partial(block_q, key_block, key_tok, value_block, value_tok, positions, limits):
    raw = jnp.einsum("rhqd,rhkd->rhqk", block_q, key_block, preferred_element_type=jnp.float32)
    scores = raw * (key_tok[:, :, None, :] * (1.0 / math.sqrt(HD)))
    visible = positions[:, None, None, :] <= limits[:, None, :, None]
    masked = jnp.where(visible, scores, NEG_FLOOR)
    top = jnp.max(masked, axis=3)
    weights = jnp.where(visible, jnp.exp(masked - top[..., None]), 0.0)
    total = jnp.sum(weights, axis=3)
    scaled = (weights * value_tok[:, :, None, :]).astype(jnp.bfloat16)
    acc = jnp.einsum("rhqk,rhkd->rhqd", scaled, value_block, preferred_element_type=jnp.float32)
    return (top, total, acc)


def round_the_ring(
    queries,
    key_codes,
    key_scale,
    value_codes,
    value_scale,
    out_weight,
    ctx_len,
    start_shard,
    draft_depth,
):
    seq_count = lax.axis_size("seq")
    here = lax.axis_index("seq")
    req_dev, rows_dev, head_dim = queries.shape
    kv_rows = key_codes.shape[2]
    group_rows = QHEADS // KVH * DRAFT
    key_tok = jnp.repeat(key_scale, BLK, axis=2)
    value_tok = jnp.repeat(value_scale, BLK, axis=2)
    offsets = jnp.mod(here - start_shard, seq_count)
    positions = offsets[:, None] * kv_rows + jnp.arange(kv_rows, dtype=jnp.int32)[None, :]
    base_limit = ctx_len - DRAFT
    draft_ids = jnp.arange(DRAFT, dtype=jnp.int32)

    def row_limits(first, count):
        draft_of = (first + jnp.arange(count, dtype=jnp.int32)) % DRAFT
        pick = (draft_of[:, None] == draft_ids[None, :]).astype(jnp.int32)
        return base_limit[:, None] + jnp.sum(draft_depth[:, None, :] * pick[None], axis=2)

    def turn(step, carry):
        block_q, top, total, acc = carry
        anchor = jnp.mod(here - step, seq_count)
        first = anchor * rows_dev
        head_pick = first // group_rows
        key_block = lax.dynamic_slice_in_dim(key_codes, head_pick, 1, 1)
        value_block = lax.dynamic_slice_in_dim(value_codes, head_pick, 1, 1)
        key_sel = lax.dynamic_slice_in_dim(key_tok, head_pick, 1, 1)
        value_sel = lax.dynamic_slice_in_dim(value_tok, head_pick, 1, 1)
        part = shard_partial(
            block_q[:, None],
            key_block,
            key_sel,
            value_block,
            value_sel,
            positions,
            row_limits(first, rows_dev),
        )
        merged = combine_state((top, total, acc), (part[0][:, 0], part[1][:, 0], part[2][:, 0]))
        moved = passed_along(
            (block_q.astype(jnp.float32), merged[0], merged[1], merged[2]), "seq", 1
        )
        return (moved[0].astype(jnp.bfloat16), moved[1], moved[2], moved[3])

    start_state = (
        queries,
        jnp.full((req_dev, rows_dev), NEG_FLOOR, jnp.float32),
        jnp.zeros((req_dev, rows_dev), jnp.float32),
        jnp.zeros((req_dev, rows_dev, head_dim), jnp.float32),
    )
    final = lax.fori_loop(0, seq_count, turn, start_state)
    attention = (final[3] / final[2][..., None]).astype(jnp.bfloat16)
    gathered = lax.all_gather(attention, "seq", axis=1, tiled=True)
    heads = gathered.shape[1] // DRAFT
    arranged = gathered.reshape(req_dev, heads, DRAFT, head_dim)
    width_dev = out_weight.shape[1]
    flat = jnp.transpose(arranged, (2, 0, 1, 3)).reshape(DRAFT * req_dev, heads * head_dim)
    result = jnp.dot(flat, out_weight, preferred_element_type=jnp.float32)
    summed = lax.psum_scatter(
        result.reshape(DRAFT, req_dev, width_dev), "head", scatter_dimension=0, tiled=True
    )
    return summed.astype(jnp.bfloat16)


def on_device(*arrays):
    queries, key_codes = arrays[:2]
    seq_count, head_count = lax.axis_size("seq"), lax.axis_size("head")
    req_dev, rows_dev, head_dim = queries.shape
    paired = all(count & (count - 1) == 0 for count in (seq_count, head_count))
    tiled = req_dev * rows_dev == head_dim and rows_dev % (2 * DRAFT) == 0
    whole = seq_count * rows_dev // key_codes.shape[1] % rows_dev == 0
    if paired and tiled and whole and DRAFT % head_count == 0:
        return with_kernels(*arrays)
    return round_the_ring(*arrays)


def solution(mesh):
    placed = (
        P("req", ("head", "seq"), None),
        P("req", "head", "seq", None),
        P("req", "head", "seq"),
        P("req", "head", "seq", None),
        P("req", "head", "seq"),
        P("head", "seq"),
        P("req"),
        P("req"),
        P("req", None),
    )
    return jax.shard_map(
        on_device, mesh=mesh, in_specs=placed, out_specs=P("head", "req", "seq"), check_vma=False
    )
```

```python
import functools
import math

import jax
import jax.numpy as jnp
from jax import lax
from jax.experimental import pallas as pl
from jax.experimental.pallas import tpu as pltpu
from jax.sharding import PartitionSpec as P

QHEADS = 128
KVH = 8
HD = 128
DRAFT = 4
BLK = 64

NEG_FLOOR = -1e30
STAT_ROWS = 16
MIB = 1 << 20
LONG = 20_000_000_000
SHORT = 1_000_000
GRANT = 8 * MIB
LATER_GRANT = GRANT + 136 * 1024
VMEM = pl.BlockSpec(memory_space=pltpu.VMEM)


def swapped(value, axis, step):
    count = lax.axis_size(axis)
    return lax.ppermute(value, axis, [(source, source ^ step) for source in range(count)])


def in_vmem(value):
    return pltpu.with_memory_space_constraint(value, pltpu.VMEM)


def in_hbm(value):
    return pltpu.with_memory_space_constraint(value, pltpu.HBM)


def kernel_call(kernel, out_shape, in_specs, flops, limit, scratch=()):
    return pl.pallas_call(
        kernel,
        out_shape=out_shape,
        in_specs=in_specs,
        out_specs=jax.tree.map(lambda _: VMEM, out_shape),
        scratch_shapes=list(scratch),
        cost_estimate=pl.CostEstimate(flops=flops, bytes_accessed=0, transcendentals=0),
        compiler_params=pltpu.CompilerParams(vmem_limit_bytes=limit),
    )


def three_parts(value):
    high = value.astype(jnp.bfloat16).astype(jnp.float32)
    rest = value - high
    middle = rest.astype(jnp.bfloat16).astype(jnp.float32)
    return (high, middle, rest - middle)


def attend(step, group_rows, q_ref, key_ref, value_ref, key_table, value_table, bias_ref):
    req_dev, rows_dev, head_dim = q_ref.shape
    head = (lax.axis_index("seq") ^ step) * rows_dev // group_rows
    heads = key_ref.shape[1]
    reqs = range(req_dev)
    raw = [
        lax.dot_general(
            q_ref[req],
            key_ref[req, head],
            (((1,), (1,)), ((), ())),
            preferred_element_type=jnp.float32,
        )
        for req in reqs
    ]
    copies = rows_dev // bias_ref.shape[1]
    masked = [
        raw[req] * key_table[pl.ds(req * heads + head, 1), :]
        + jnp.concatenate([bias_ref[req]] * copies, axis=0)
        for req in reqs
    ]
    top = [jnp.max(part, axis=1, keepdims=True) for part in masked]
    weights = [jnp.exp2(part - high) for part, high in zip(masked, top)]
    total = [
        jnp.where(high > 0.5 * NEG_FLOOR, jnp.sum(part, axis=1, keepdims=True), 0.0)
        for part, high in zip(weights, top)
    ]
    scaled = [
        (weights[req] * value_table[pl.ds(req * heads + head, 1), :]).astype(jnp.bfloat16)
        for req in reqs
    ]
    acc = [
        jnp.dot(scaled[req], value_ref[req, head], preferred_element_type=jnp.float32)
        for req in reqs
    ]
    return [jnp.concatenate(parts, axis=0) for parts in (acc, top, total)]


def prepare_kernel(head_dim, *refs):
    given, refs = refs[:8], refs[8:]
    key_ref, value_ref, key_table, value_table, bias_ref, q_ref = refs[:6]
    ctx, start, depth, key_scale, value_scale, sems = refs[6:]
    targets = (ctx, start, depth, key_scale, value_scale, key_ref, value_ref, q_ref)
    copies = [
        pltpu.make_async_copy(source, target, sems.at[at])
        for at, (source, target) in enumerate(zip(given, targets))
    ]
    for copy in copies:
        copy.start()
    req_dev, heads, kv_rows = key_ref.shape[:3]
    blocks = key_scale.shape[2]
    width = kv_rows // blocks
    drafts = depth.shape[1]
    seq_count = lax.axis_size("seq")
    here = lax.axis_index("seq")
    lane = lax.broadcasted_iota(jnp.int32, (1, kv_rows), 1)
    tall = bias_ref.shape[1]
    draft_of = lax.broadcasted_iota(jnp.int32, (tall, kv_rows), 0) % drafts
    for copy in copies[:5]:
        copy.wait()
    factor = math.log2(math.e) / math.sqrt(head_dim)
    for scale, table, by in ((key_scale, key_table, factor), (value_scale, value_table, 1.0)):
        scales = jnp.concatenate([scale[req] for req in range(req_dev)], axis=0) * by
        found = jnp.broadcast_to(scales[:, :1], table.shape)
        for block in range(1, blocks):
            found = jnp.where(lane >= block * width, scales[:, block : block + 1], found)
        table[...] = found
    for req in range(req_dev):
        first = jnp.where(here >= start[req], here - start[req], here - start[req] + seq_count)
        limit = jnp.full((tall, kv_rows), depth[req, 0], jnp.int32)
        for draft in range(1, drafts):
            limit = jnp.where(draft_of == draft, depth[req, draft], limit)
        limit = limit + (ctx[req] - drafts - first * kv_rows)
        bias_ref[req] = jnp.where(lane <= limit, 0.0, NEG_FLOOR)
    for copy in copies[5:]:
        copy.wait()


def attend_kernel(steps, group_rows, *refs):
    count = len(steps)
    out_ref = refs[-1]
    parts = [
        attend(step, group_rows, q_ref, *refs[count : count + 5])
        for step, q_ref in zip(steps, refs[:count])
    ]
    rows, lanes = parts[0][0].shape
    lane = lax.broadcasted_iota(jnp.int32, (rows, lanes), 1)
    stats = jnp.zeros((rows, lanes), jnp.float32)
    for at, (acc, top, total) in enumerate(parts):
        out_ref[at * rows : (at + 1) * rows, :] = acc.astype(jnp.bfloat16)
        stats = jnp.where(lane == 2 * at, top, jnp.where(lane == 2 * at + 1, total, stats))
    turned = jnp.transpose(stats)
    found = [part for at in range(2 * count) for part in three_parts(turned[at : at + 1])]
    spare = out_ref.shape[0] - rows * count - len(found)
    found.append(jnp.zeros((spare, lanes), jnp.float32))
    out_ref[rows * count :, :] = jnp.concatenate(found, axis=0).astype(jnp.bfloat16)


def kept_steps(count):
    return [step for step in range(count) if step % 2 == 0]


def stat_rows(count):
    return -(-6 * count // STAT_ROWS) * STAT_ROWS


def read_stats(ref, first):
    stats = ref[first:, :].astype(jnp.float32)
    return [
        (
            stats[at : at + 1] + stats[at + 1 : at + 2] + stats[at + 2 : at + 3],
            stats[at + 3 : at + 4] + stats[at + 4 : at + 5] + stats[at + 5 : at + 6],
        )
        for at in range(0, stats.shape[0] - 5, 6)
    ]


def combine_stats(stats):
    top = functools.reduce(jnp.maximum, [part[0] for part in stats])
    factors = [jnp.exp2(part[0] - top) for part in stats]
    total = sum(part[1] * factor for part, factor in zip(stats, factors))
    return top, total, factors


def as_columns(rows):
    lanes = rows[0].shape[1]
    which = lax.broadcasted_iota(jnp.int32, (lanes, lanes), 0)
    table = jnp.zeros((lanes, lanes), jnp.float32)
    for at, row in enumerate(rows):
        table = jnp.where(which == at, row, table)
    turned = jnp.transpose(table)
    return [turned[:, at : at + 1] for at in range(len(rows))]


def pair_kernel(rows, kept, *refs):
    sides, out_ref = refs[:2], refs[-1]
    stats = [read_stats(ref, rows * kept) for ref in sides]
    found, columns = [], []
    for at in range(kept):
        top, total, factors = combine_stats([stat[at] for stat in stats])
        found += [*three_parts(top), *three_parts(total)]
        columns += factors
    columns = as_columns(columns)
    merged = [
        sum(
            ref[at * rows : (at + 1) * rows, :].astype(jnp.float32) * columns[2 * at + side]
            for side, ref in enumerate(sides)
        )
        for at in range(kept)
    ]
    spare = out_ref.shape[0] - rows * kept - len(found)
    found.append(jnp.zeros((spare, out_ref.shape[1]), jnp.float32))
    for at, part in enumerate(merged):
        out_ref[at * rows : (at + 1) * rows, :] = part.astype(jnp.bfloat16)
    out_ref[rows * kept :, :] = jnp.concatenate(found, axis=0).astype(jnp.bfloat16)


def merged_blocks(group, kept, rows_dev, drafts, part_refs, held, ordered):
    rows = (part_refs[0].shape[0] - stat_rows(len(kept))) // len(kept)
    req_dev = rows // rows_dev
    heads = rows_dev // drafts
    lines = drafts * req_dev
    share = drafts // lax.axis_size("head")
    mine = lax.axis_index("head")
    stats = [read_stats(ref, rows * len(kept)) for ref in part_refs]
    places = [[kept.index(block ^ peer) for peer in group] for block in group]
    table = []
    for place in places:
        _, total, factors = combine_stats([stat[at] for stat, at in zip(stats, place)])
        table += [factor / total for factor in factors]
    columns = iter(as_columns(table))
    for block, place in enumerate(places):
        held[block, :rows, :] = sum(
            ref[at * rows : (at + 1) * rows, :].astype(jnp.float32) * next(columns)
            for ref, at in zip(part_refs, place)
        )
    for block in range(len(group)):
        for req in range(req_dev):
            for draft in range(drafts):
                taken = held[block, pl.ds(req * rows_dev + draft, heads, stride=drafts), :]
                place = (draft // share) ^ mine
                row = (place * share + draft % share) * req_dev + req
                ordered[block, pl.ds(row, heads, stride=lines), :] = taken
    return [
        jnp.concatenate(
            [ordered[block, head * lines : (head + 1) * lines, :] for head in range(heads)], axis=1
        ).astype(jnp.bfloat16)
        for block in range(len(group))
    ]


def project_kernel(group, kept, rows_dev, drafts, first, *refs):
    count = len(group)
    part_refs, weight_ref = refs[:count], refs[count]
    before = None if first else refs[count + 1]
    out_refs = refs[count + 1 if first else count + 2 : -2]
    parts = merged_blocks(group, kept, rows_dev, drafts, part_refs, *refs[-2:])
    here = lax.axis_index("seq")
    depth = weight_ref.shape[0] // lax.axis_size("seq")
    wide = weight_ref.shape[1]
    cut = min(wide, 512)
    tall = out_refs[0].shape[0]
    for column in range(0, wide, cut):
        spot = slice(column, column + cut)
        found = None if first else before[:, spot]
        for step, part in zip(group, parts):
            start = pl.multiple_of((here ^ step) * depth, depth)
            product = jnp.dot(
                part, weight_ref[pl.ds(start, depth), spot], preferred_element_type=jnp.float32
            )
            found = product if found is None else found + product
        for piece, out_ref in enumerate(out_refs):
            out_ref[:, spot] = found[piece * tall : (piece + 1) * tall].astype(out_ref.dtype)


def sum_kernel(*refs):
    out_ref = refs[-1]
    total = refs[0][...].astype(jnp.float32)
    for ref in refs[1:-1]:
        total = total + ref[...].astype(jnp.float32)
    out_ref[...] = total.astype(out_ref.dtype).reshape(out_ref.shape)


def with_kernels(
    queries,
    key_codes,
    key_scale,
    value_codes,
    value_scale,
    out_weight,
    ctx_len,
    start_shard,
    draft_depth,
):
    seq_count = lax.axis_size("seq")
    head_count = lax.axis_size("head")
    req_dev, rows_dev, head_dim = queries.shape
    group_rows = seq_count * rows_dev // key_codes.shape[1]
    drafts = draft_depth.shape[1]
    rows = req_dev * rows_dev
    wide = out_weight.shape[1]
    others = range(1, seq_count)
    kv_heads, kv_rows = key_codes.shape[1:3]
    tall = 2 * drafts
    given = (
        ctx_len,
        start_shard,
        draft_depth,
        key_scale,
        value_scale,
        key_codes,
        value_codes,
        queries,
    )
    *tables, own_queries = kernel_call(
        functools.partial(prepare_kernel, head_dim),
        [
            pltpu.VMEM(key_codes.shape, key_codes.dtype),
            pltpu.VMEM(value_codes.shape, value_codes.dtype),
            pltpu.VMEM((req_dev * kv_heads, kv_rows), jnp.float32),
            pltpu.VMEM((req_dev * kv_heads, kv_rows), jnp.float32),
            pltpu.VMEM((req_dev, tall, kv_rows), jnp.float32),
            pltpu.VMEM(queries.shape, queries.dtype),
        ],
        [pl.BlockSpec(memory_space=pltpu.HBM)] * len(given),
        SHORT,
        8 * MIB,
        [pltpu.SMEM(part.shape, part.dtype) for part in given[:3]]
        + [pltpu.VMEM(part.shape, part.dtype) for part in given[3:5]]
        + [pltpu.SemaphoreType.DMA((len(given),))],
    )(*map(in_hbm, given))

    def partial(steps, flops):
        return kernel_call(
            functools.partial(attend_kernel, steps, group_rows),
            pltpu.VMEM((len(steps) * rows + stat_rows(len(steps)), head_dim), jnp.bfloat16),
            [VMEM] * (len(steps) + len(tables)),
            flops,
            4 * MIB,
        )(*[blocks[step] for step in steps], *tables)

    blocks = {step: swapped(queries, "seq", step) for step in others} | {0: own_queries}
    kept = kept_steps(seq_count)
    handed = partial([step ^ 1 for step in kept], LONG)
    returned = swapped(handed, "seq", 1)
    mine = partial(kept, LONG)
    paired = kernel_call(
        functools.partial(pair_kernel, rows, len(kept)),
        pltpu.VMEM((rows * len(kept) + stat_rows(len(kept)), head_dim), jnp.bfloat16),
        [VMEM] * 2,
        SHORT,
        4 * MIB,
    )(mine, returned)
    gathered = dict(enumerate([paired] + [swapped(paired, "seq", step) for step in others]))
    weights = in_vmem(out_weight)
    lines = drafts * req_dev
    running = ()
    for group in (kept, [step for step in range(seq_count) if step not in kept]):
        first = not running
        running = kernel_call(
            functools.partial(project_kernel, group, kept, rows_dev, drafts, first),
            [pltpu.VMEM((lines, wide), jnp.float32)]
            if first
            else [pltpu.VMEM((lines // head_count, wide), jnp.bfloat16)] * head_count,
            [VMEM] * (len(group) + 1 + len(running)),
            SHORT,
            GRANT if first else LATER_GRANT,
            [pltpu.VMEM((len(group), rows + lines, head_dim), jnp.float32)] * 2,
        )(*[gathered[step] for step in group], weights, *running)
    shares = running
    summed = [swapped(shares[step], "head", step) for step in range(head_count - 1, 0, -1)]
    return kernel_call(
        sum_kernel,
        jax.ShapeDtypeStruct((drafts // head_count, req_dev, wide), jnp.bfloat16),
        [VMEM] * head_count,
        SHORT,
        4 * MIB,
    )(shares[0], *summed)


def passed_along(value, axis, steps):
    count = lax.axis_size(axis)
    pairs = [(source, (source + steps) % count) for source in range(count)]
    return lax.ppermute(value, axis, pairs)


def combine_state(first, second):
    top = jnp.maximum(first[0], second[0])
    early = jnp.exp(first[0] - top)
    later = jnp.exp(second[0] - top)
    return (
        top,
        first[1] * early + second[1] * later,
        first[2] * early[..., None] + second[2] * later[..., None],
    )


def shard_partial(block_q, key_block, key_tok, value_block, value_tok, positions, limits):
    raw = jnp.einsum("rhqd,rhkd->rhqk", block_q, key_block, preferred_element_type=jnp.float32)
    scores = raw * (key_tok[:, :, None, :] * (1.0 / math.sqrt(HD)))
    visible = positions[:, None, None, :] <= limits[:, None, :, None]
    masked = jnp.where(visible, scores, NEG_FLOOR)
    top = jnp.max(masked, axis=3)
    weights = jnp.where(visible, jnp.exp(masked - top[..., None]), 0.0)
    total = jnp.sum(weights, axis=3)
    scaled = (weights * value_tok[:, :, None, :]).astype(jnp.bfloat16)
    acc = jnp.einsum("rhqk,rhkd->rhqd", scaled, value_block, preferred_element_type=jnp.float32)
    return (top, total, acc)


def round_the_ring(
    queries,
    key_codes,
    key_scale,
    value_codes,
    value_scale,
    out_weight,
    ctx_len,
    start_shard,
    draft_depth,
):
    seq_count = lax.axis_size("seq")
    here = lax.axis_index("seq")
    req_dev, rows_dev, head_dim = queries.shape
    kv_rows = key_codes.shape[2]
    group_rows = QHEADS // KVH * DRAFT
    key_tok = jnp.repeat(key_scale, BLK, axis=2)
    value_tok = jnp.repeat(value_scale, BLK, axis=2)
    offsets = jnp.mod(here - start_shard, seq_count)
    positions = offsets[:, None] * kv_rows + jnp.arange(kv_rows, dtype=jnp.int32)[None, :]
    base_limit = ctx_len - DRAFT
    draft_ids = jnp.arange(DRAFT, dtype=jnp.int32)

    def row_limits(first, count):
        draft_of = (first + jnp.arange(count, dtype=jnp.int32)) % DRAFT
        pick = (draft_of[:, None] == draft_ids[None, :]).astype(jnp.int32)
        return base_limit[:, None] + jnp.sum(draft_depth[:, None, :] * pick[None], axis=2)

    def turn(step, carry):
        block_q, top, total, acc = carry
        anchor = jnp.mod(here - step, seq_count)
        first = anchor * rows_dev
        head_pick = first // group_rows
        key_block = lax.dynamic_slice_in_dim(key_codes, head_pick, 1, 1)
        value_block = lax.dynamic_slice_in_dim(value_codes, head_pick, 1, 1)
        key_sel = lax.dynamic_slice_in_dim(key_tok, head_pick, 1, 1)
        value_sel = lax.dynamic_slice_in_dim(value_tok, head_pick, 1, 1)
        part = shard_partial(
            block_q[:, None],
            key_block,
            key_sel,
            value_block,
            value_sel,
            positions,
            row_limits(first, rows_dev),
        )
        merged = combine_state((top, total, acc), (part[0][:, 0], part[1][:, 0], part[2][:, 0]))
        moved = passed_along(
            (block_q.astype(jnp.float32), merged[0], merged[1], merged[2]), "seq", 1
        )
        return (moved[0].astype(jnp.bfloat16), moved[1], moved[2], moved[3])

    start_state = (
        queries,
        jnp.full((req_dev, rows_dev), NEG_FLOOR, jnp.float32),
        jnp.zeros((req_dev, rows_dev), jnp.float32),
        jnp.zeros((req_dev, rows_dev, head_dim), jnp.float32),
    )
    final = lax.fori_loop(0, seq_count, turn, start_state)
    attention = (final[3] / final[2][..., None]).astype(jnp.bfloat16)
    gathered = lax.all_gather(attention, "seq", axis=1, tiled=True)
    heads = gathered.shape[1] // DRAFT
    arranged = gathered.reshape(req_dev, heads, DRAFT, head_dim)
    width_dev = out_weight.shape[1]
    flat = jnp.transpose(arranged, (2, 0, 1, 3)).reshape(DRAFT * req_dev, heads * head_dim)
    result = jnp.dot(flat, out_weight, preferred_element_type=jnp.float32)
    summed = lax.psum_scatter(
        result.reshape(DRAFT, req_dev, width_dev), "head", scatter_dimension=0, tiled=True
    )
    return summed.astype(jnp.bfloat16)


def on_device(*arrays):
    queries, key_codes = arrays[:2]
    seq_count, head_count = lax.axis_size("seq"), lax.axis_size("head")
    req_dev, rows_dev, head_dim = queries.shape
    paired = all(count & (count - 1) == 0 for count in (seq_count, head_count))
    tiled = req_dev * rows_dev == head_dim and rows_dev % (2 * DRAFT) == 0
    whole = seq_count * rows_dev // key_codes.shape[1] % rows_dev == 0
    if paired and tiled and whole and DRAFT % head_count == 0:
        return with_kernels(*arrays)
    return round_the_ring(*arrays)


def solution(mesh):
    placed = (
        P("req", ("head", "seq"), None),
        P("req", "head", "seq", None),
        P("req", "head", "seq"),
        P("req", "head", "seq", None),
        P("req", "head", "seq"),
        P("head", "seq"),
        P("req"),
        P("req"),
        P("req", None),
    )
    return jax.shard_map(
        on_device, mesh=mesh, in_specs=placed, out_specs=P("head", "req", "seq"), check_vma=False
    )
```

```python
import functools
import math

import jax
import jax.numpy as jnp
from jax import lax
from jax.experimental import pallas as pl
from jax.experimental.pallas import tpu as pltpu
from jax.sharding import PartitionSpec as P

QHEADS = 128
KVH = 8
HD = 128
DRAFT = 4
BLK = 64

NEG_FLOOR = -1e30
STAT_ROWS = 16
MIB = 1 << 20
LONG = 20_000_000_000
SHORT = 1_000_000
GRANT = 8 * MIB
LATER_GRANT = GRANT + 136 * 1024
VMEM = pl.BlockSpec(memory_space=pltpu.VMEM)


def swapped(value, axis, step):
    count = lax.axis_size(axis)
    return lax.ppermute(value, axis, [(source, source ^ step) for source in range(count)])


def in_vmem(value):
    return pltpu.with_memory_space_constraint(value, pltpu.VMEM)


def in_hbm(value):
    return pltpu.with_memory_space_constraint(value, pltpu.HBM)


def kernel_call(kernel, out_shape, in_specs, flops, limit, scratch=()):
    return pl.pallas_call(
        kernel,
        out_shape=out_shape,
        in_specs=in_specs,
        out_specs=jax.tree.map(lambda _: VMEM, out_shape),
        scratch_shapes=list(scratch),
        cost_estimate=pl.CostEstimate(flops=flops, bytes_accessed=0, transcendentals=0),
        compiler_params=pltpu.CompilerParams(vmem_limit_bytes=limit),
    )


def three_parts(value):
    high = value.astype(jnp.bfloat16).astype(jnp.float32)
    rest = value - high
    middle = rest.astype(jnp.bfloat16).astype(jnp.float32)
    return (high, middle, rest - middle)


def attend(step, group_rows, q_ref, key_ref, value_ref, key_table, value_table, bias_ref):
    req_dev, rows_dev, head_dim = q_ref.shape
    head = (lax.axis_index("seq") ^ step) * rows_dev // group_rows
    heads = key_ref.shape[1]
    reqs = range(req_dev)
    raw = [
        lax.dot_general(
            q_ref[req],
            key_ref[req, head],
            (((1,), (1,)), ((), ())),
            preferred_element_type=jnp.float32,
        )
        for req in reqs
    ]
    copies = rows_dev // bias_ref.shape[1]
    masked = [
        raw[req] * key_table[pl.ds(req * heads + head, 1), :]
        + jnp.concatenate([bias_ref[req]] * copies, axis=0)
        for req in reqs
    ]
    top = [jnp.max(part, axis=1, keepdims=True) for part in masked]
    weights = [jnp.exp2(part - high) for part, high in zip(masked, top)]
    total = [
        jnp.where(high > 0.5 * NEG_FLOOR, jnp.sum(part, axis=1, keepdims=True), 0.0)
        for part, high in zip(weights, top)
    ]
    scaled = [
        (weights[req] * value_table[pl.ds(req * heads + head, 1), :]).astype(jnp.bfloat16)
        for req in reqs
    ]
    acc = [
        jnp.dot(scaled[req], value_ref[req, head], preferred_element_type=jnp.float32)
        for req in reqs
    ]
    return [jnp.concatenate(parts, axis=0) for parts in (acc, top, total)]


def prepare_kernel(head_dim, *refs):
    given, refs = refs[:8], refs[8:]
    key_ref, value_ref, key_table, value_table, bias_ref, q_ref = refs[:6]
    ctx, start, depth, key_scale, value_scale, sems = refs[6:]
    targets = (ctx, start, depth, key_scale, value_scale, key_ref, value_ref, q_ref)
    copies = [
        pltpu.make_async_copy(source, target, sems.at[at])
        for at, (source, target) in enumerate(zip(given, targets))
    ]
    for copy in copies[5:] + copies[:5]:
        copy.start()
    req_dev, heads, kv_rows = key_ref.shape[:3]
    blocks = key_scale.shape[2]
    width = kv_rows // blocks
    drafts = depth.shape[1]
    seq_count = lax.axis_size("seq")
    here = lax.axis_index("seq")
    lane = lax.broadcasted_iota(jnp.int32, (1, kv_rows), 1)
    tall = bias_ref.shape[1]
    draft_of = lax.broadcasted_iota(jnp.int32, (tall, kv_rows), 0) % drafts
    for copy in copies[:5]:
        copy.wait()
    factor = math.log2(math.e) / math.sqrt(head_dim)
    for scale, table, by in ((key_scale, key_table, factor), (value_scale, value_table, 1.0)):
        scales = jnp.concatenate([scale[req] for req in range(req_dev)], axis=0) * by
        found = jnp.broadcast_to(scales[:, :1], table.shape)
        for block in range(1, blocks):
            found = jnp.where(lane >= block * width, scales[:, block : block + 1], found)
        table[...] = found
    for req in range(req_dev):
        first = jnp.where(here >= start[req], here - start[req], here - start[req] + seq_count)
        limit = jnp.full((tall, kv_rows), depth[req, 0], jnp.int32)
        for draft in range(1, drafts):
            limit = jnp.where(draft_of == draft, depth[req, draft], limit)
        limit = limit + (ctx[req] - drafts - first * kv_rows)
        bias_ref[req] = jnp.where(lane <= limit, 0.0, NEG_FLOOR)
    for copy in copies[5:]:
        copy.wait()


def attend_kernel(steps, group_rows, *refs):
    count = len(steps)
    out_ref = refs[-1]
    parts = [
        attend(step, group_rows, q_ref, *refs[count : count + 5])
        for step, q_ref in zip(steps, refs[:count])
    ]
    rows, lanes = parts[0][0].shape
    lane = lax.broadcasted_iota(jnp.int32, (rows, lanes), 1)
    stats = jnp.zeros((rows, lanes), jnp.float32)
    for at, (acc, top, total) in enumerate(parts):
        out_ref[at * rows : (at + 1) * rows, :] = acc.astype(jnp.bfloat16)
        stats = jnp.where(lane == 2 * at, top, jnp.where(lane == 2 * at + 1, total, stats))
    turned = jnp.transpose(stats)
    found = [part for at in range(2 * count) for part in three_parts(turned[at : at + 1])]
    spare = out_ref.shape[0] - rows * count - len(found)
    found.append(jnp.zeros((spare, lanes), jnp.float32))
    out_ref[rows * count :, :] = jnp.concatenate(found, axis=0).astype(jnp.bfloat16)


def kept_steps(count):
    return [step for step in range(count) if step % 2 == 0]


def stat_rows(count):
    return -(-6 * count // STAT_ROWS) * STAT_ROWS


def read_stats(ref, first):
    stats = ref[first:, :].astype(jnp.float32)
    return [
        (
            stats[at : at + 1] + stats[at + 1 : at + 2] + stats[at + 2 : at + 3],
            stats[at + 3 : at + 4] + stats[at + 4 : at + 5] + stats[at + 5 : at + 6],
        )
        for at in range(0, stats.shape[0] - 5, 6)
    ]


def combine_stats(stats):
    top = functools.reduce(jnp.maximum, [part[0] for part in stats])
    factors = [jnp.exp2(part[0] - top) for part in stats]
    total = sum(part[1] * factor for part, factor in zip(stats, factors))
    return top, total, factors


def as_columns(rows):
    lanes = rows[0].shape[1]
    spare = -len(rows) % 8
    table = jnp.concatenate([*rows, jnp.zeros((spare, lanes), jnp.float32)], axis=0)
    turned = jnp.transpose(table)
    return [turned[:, at : at + 1] for at in range(len(rows))]


def pair_kernel(rows, kept, *refs):
    sides, out_ref = refs[:2], refs[-1]
    stats = [read_stats(ref, rows * kept) for ref in sides]
    found, columns = [], []
    for at in range(kept):
        top, total, factors = combine_stats([stat[at] for stat in stats])
        found += [*three_parts(top), *three_parts(total)]
        columns += factors
    columns = as_columns(columns)
    merged = [
        sum(
            ref[at * rows : (at + 1) * rows, :].astype(jnp.float32) * columns[2 * at + side]
            for side, ref in enumerate(sides)
        )
        for at in range(kept)
    ]
    spare = out_ref.shape[0] - rows * kept - len(found)
    found.append(jnp.zeros((spare, out_ref.shape[1]), jnp.float32))
    for at, part in enumerate(merged):
        out_ref[at * rows : (at + 1) * rows, :] = part.astype(jnp.bfloat16)
    out_ref[rows * kept :, :] = jnp.concatenate(found, axis=0).astype(jnp.bfloat16)


def merged_blocks(group, kept, rows_dev, drafts, part_refs, held, ordered):
    rows = (part_refs[0].shape[0] - stat_rows(len(kept))) // len(kept)
    req_dev = rows // rows_dev
    heads = rows_dev // drafts
    lines = drafts * req_dev
    share = drafts // lax.axis_size("head")
    mine = lax.axis_index("head")
    stats = [read_stats(ref, rows * len(kept)) for ref in part_refs]
    places = [[kept.index(block ^ peer) for peer in group] for block in group]
    table = []
    for place in places:
        _, total, factors = combine_stats([stat[at] for stat, at in zip(stats, place)])
        table += [factor / total for factor in factors]
    columns = iter(as_columns(table))
    for block, place in enumerate(places):
        held[block, :rows, :] = sum(
            ref[at * rows : (at + 1) * rows, :].astype(jnp.float32) * next(columns)
            for ref, at in zip(part_refs, place)
        )
    for block in range(len(group)):
        for req in range(req_dev):
            for draft in range(drafts):
                taken = held[block, pl.ds(req * rows_dev + draft, heads, stride=drafts), :]
                place = (draft // share) ^ mine
                row = (place * share + draft % share) * req_dev + req
                ordered[block, pl.ds(row, heads, stride=lines), :] = taken
    return [
        jnp.concatenate(
            [ordered[block, head * lines : (head + 1) * lines, :] for head in range(heads)], axis=1
        ).astype(jnp.bfloat16)
        for block in range(len(group))
    ]


def project_kernel(group, kept, rows_dev, drafts, first, *refs):
    count = len(group)
    part_refs, weight_ref = refs[:count], refs[count]
    before = None if first else refs[count + 1]
    out_refs = refs[count + 1 if first else count + 2 : -2]
    parts = merged_blocks(group, kept, rows_dev, drafts, part_refs, *refs[-2:])
    here = lax.axis_index("seq")
    depth = weight_ref.shape[0] // lax.axis_size("seq")
    wide = weight_ref.shape[1]
    cut = min(wide, 512)
    tall = out_refs[0].shape[0]
    for column in range(0, wide, cut):
        spot = slice(column, column + cut)
        found = None if first else before[:, spot]
        for step, part in zip(group, parts):
            start = pl.multiple_of((here ^ step) * depth, depth)
            product = jnp.dot(
                part, weight_ref[pl.ds(start, depth), spot], preferred_element_type=jnp.float32
            )
            found = product if found is None else found + product
        for piece, out_ref in enumerate(out_refs):
            out_ref[:, spot] = found[piece * tall : (piece + 1) * tall].astype(out_ref.dtype)


def sum_kernel(*refs):
    out_ref = refs[-1]
    total = refs[0][...].astype(jnp.float32)
    for ref in refs[1:-1]:
        total = total + ref[...].astype(jnp.float32)
    out_ref[...] = total.astype(out_ref.dtype).reshape(out_ref.shape)


def with_kernels(
    queries,
    key_codes,
    key_scale,
    value_codes,
    value_scale,
    out_weight,
    ctx_len,
    start_shard,
    draft_depth,
):
    seq_count = lax.axis_size("seq")
    head_count = lax.axis_size("head")
    req_dev, rows_dev, head_dim = queries.shape
    group_rows = seq_count * rows_dev // key_codes.shape[1]
    drafts = draft_depth.shape[1]
    rows = req_dev * rows_dev
    wide = out_weight.shape[1]
    others = range(1, seq_count)
    kv_heads, kv_rows = key_codes.shape[1:3]
    tall = 2 * drafts
    given = (
        ctx_len,
        start_shard,
        draft_depth,
        key_scale,
        value_scale,
        key_codes,
        value_codes,
        queries,
    )
    *tables, own_queries = kernel_call(
        functools.partial(prepare_kernel, head_dim),
        [
            pltpu.VMEM(key_codes.shape, key_codes.dtype),
            pltpu.VMEM(value_codes.shape, value_codes.dtype),
            pltpu.VMEM((req_dev * kv_heads, kv_rows), jnp.float32),
            pltpu.VMEM((req_dev * kv_heads, kv_rows), jnp.float32),
            pltpu.VMEM((req_dev, tall, kv_rows), jnp.float32),
            pltpu.VMEM(queries.shape, queries.dtype),
        ],
        [pl.BlockSpec(memory_space=pltpu.HBM)] * len(given),
        SHORT,
        8 * MIB,
        [pltpu.SMEM(part.shape, part.dtype) for part in given[:3]]
        + [pltpu.VMEM(part.shape, part.dtype) for part in given[3:5]]
        + [pltpu.SemaphoreType.DMA((len(given),))],
    )(*map(in_hbm, given))

    def partial(steps, flops):
        return kernel_call(
            functools.partial(attend_kernel, steps, group_rows),
            pltpu.VMEM((len(steps) * rows + stat_rows(len(steps)), head_dim), jnp.bfloat16),
            [VMEM] * (len(steps) + len(tables)),
            flops,
            4 * MIB,
        )(*[blocks[step] for step in steps], *tables)

    blocks = {step: swapped(queries, "seq", step) for step in others} | {0: own_queries}
    kept = kept_steps(seq_count)
    handed = partial([step ^ 1 for step in kept], LONG)
    returned = swapped(handed, "seq", 1)
    mine = partial(kept, LONG)
    paired = kernel_call(
        functools.partial(pair_kernel, rows, len(kept)),
        pltpu.VMEM((rows * len(kept) + stat_rows(len(kept)), head_dim), jnp.bfloat16),
        [VMEM] * 2,
        SHORT,
        4 * MIB,
    )(mine, returned)
    gathered = dict(enumerate([paired] + [swapped(paired, "seq", step) for step in others]))
    weights = in_vmem(out_weight)
    lines = drafts * req_dev
    running = ()
    for group in (kept, [step for step in range(seq_count) if step not in kept]):
        first = not running
        running = kernel_call(
            functools.partial(project_kernel, group, kept, rows_dev, drafts, first),
            [pltpu.VMEM((lines, wide), jnp.float32)]
            if first
            else [pltpu.VMEM((lines // head_count, wide), jnp.bfloat16)] * head_count,
            [VMEM] * (len(group) + 1 + len(running)),
            SHORT,
            GRANT if first else LATER_GRANT,
            [pltpu.VMEM((len(group), rows + lines, head_dim), jnp.float32)] * 2,
        )(*[gathered[step] for step in group], weights, *running)
    shares = running
    summed = [swapped(shares[step], "head", step) for step in range(head_count - 1, 0, -1)]
    return kernel_call(
        sum_kernel,
        jax.ShapeDtypeStruct((drafts // head_count, req_dev, wide), jnp.bfloat16),
        [VMEM] * head_count,
        SHORT,
        4 * MIB,
    )(shares[0], *summed)


def passed_along(value, axis, steps):
    count = lax.axis_size(axis)
    pairs = [(source, (source + steps) % count) for source in range(count)]
    return lax.ppermute(value, axis, pairs)


def combine_state(first, second):
    top = jnp.maximum(first[0], second[0])
    early = jnp.exp(first[0] - top)
    later = jnp.exp(second[0] - top)
    return (
        top,
        first[1] * early + second[1] * later,
        first[2] * early[..., None] + second[2] * later[..., None],
    )


def shard_partial(block_q, key_block, key_tok, value_block, value_tok, positions, limits):
    raw = jnp.einsum("rhqd,rhkd->rhqk", block_q, key_block, preferred_element_type=jnp.float32)
    scores = raw * (key_tok[:, :, None, :] * (1.0 / math.sqrt(HD)))
    visible = positions[:, None, None, :] <= limits[:, None, :, None]
    masked = jnp.where(visible, scores, NEG_FLOOR)
    top = jnp.max(masked, axis=3)
    weights = jnp.where(visible, jnp.exp(masked - top[..., None]), 0.0)
    total = jnp.sum(weights, axis=3)
    scaled = (weights * value_tok[:, :, None, :]).astype(jnp.bfloat16)
    acc = jnp.einsum("rhqk,rhkd->rhqd", scaled, value_block, preferred_element_type=jnp.float32)
    return (top, total, acc)


def round_the_ring(
    queries,
    key_codes,
    key_scale,
    value_codes,
    value_scale,
    out_weight,
    ctx_len,
    start_shard,
    draft_depth,
):
    seq_count = lax.axis_size("seq")
    here = lax.axis_index("seq")
    req_dev, rows_dev, head_dim = queries.shape
    kv_rows = key_codes.shape[2]
    group_rows = QHEADS // KVH * DRAFT
    key_tok = jnp.repeat(key_scale, BLK, axis=2)
    value_tok = jnp.repeat(value_scale, BLK, axis=2)
    offsets = jnp.mod(here - start_shard, seq_count)
    positions = offsets[:, None] * kv_rows + jnp.arange(kv_rows, dtype=jnp.int32)[None, :]
    base_limit = ctx_len - DRAFT
    draft_ids = jnp.arange(DRAFT, dtype=jnp.int32)

    def row_limits(first, count):
        draft_of = (first + jnp.arange(count, dtype=jnp.int32)) % DRAFT
        pick = (draft_of[:, None] == draft_ids[None, :]).astype(jnp.int32)
        return base_limit[:, None] + jnp.sum(draft_depth[:, None, :] * pick[None], axis=2)

    def turn(step, carry):
        block_q, top, total, acc = carry
        anchor = jnp.mod(here - step, seq_count)
        first = anchor * rows_dev
        head_pick = first // group_rows
        key_block = lax.dynamic_slice_in_dim(key_codes, head_pick, 1, 1)
        value_block = lax.dynamic_slice_in_dim(value_codes, head_pick, 1, 1)
        key_sel = lax.dynamic_slice_in_dim(key_tok, head_pick, 1, 1)
        value_sel = lax.dynamic_slice_in_dim(value_tok, head_pick, 1, 1)
        part = shard_partial(
            block_q[:, None],
            key_block,
            key_sel,
            value_block,
            value_sel,
            positions,
            row_limits(first, rows_dev),
        )
        merged = combine_state((top, total, acc), (part[0][:, 0], part[1][:, 0], part[2][:, 0]))
        moved = passed_along(
            (block_q.astype(jnp.float32), merged[0], merged[1], merged[2]), "seq", 1
        )
        return (moved[0].astype(jnp.bfloat16), moved[1], moved[2], moved[3])

    start_state = (
        queries,
        jnp.full((req_dev, rows_dev), NEG_FLOOR, jnp.float32),
        jnp.zeros((req_dev, rows_dev), jnp.float32),
        jnp.zeros((req_dev, rows_dev, head_dim), jnp.float32),
    )
    final = lax.fori_loop(0, seq_count, turn, start_state)
    attention = (final[3] / final[2][..., None]).astype(jnp.bfloat16)
    gathered = lax.all_gather(attention, "seq", axis=1, tiled=True)
    heads = gathered.shape[1] // DRAFT
    arranged = gathered.reshape(req_dev, heads, DRAFT, head_dim)
    width_dev = out_weight.shape[1]
    flat = jnp.transpose(arranged, (2, 0, 1, 3)).reshape(DRAFT * req_dev, heads * head_dim)
    result = jnp.dot(flat, out_weight, preferred_element_type=jnp.float32)
    summed = lax.psum_scatter(
        result.reshape(DRAFT, req_dev, width_dev), "head", scatter_dimension=0, tiled=True
    )
    return summed.astype(jnp.bfloat16)


def on_device(*arrays):
    queries, key_codes = arrays[:2]
    seq_count, head_count = lax.axis_size("seq"), lax.axis_size("head")
    req_dev, rows_dev, head_dim = queries.shape
    paired = all(count & (count - 1) == 0 for count in (seq_count, head_count))
    tiled = req_dev * rows_dev == head_dim and rows_dev % (2 * DRAFT) == 0
    whole = seq_count * rows_dev // key_codes.shape[1] % rows_dev == 0
    if paired and tiled and whole and DRAFT % head_count == 0:
        return with_kernels(*arrays)
    return round_the_ring(*arrays)


def solution(mesh):
    placed = (
        P("req", ("head", "seq"), None),
        P("req", "head", "seq", None),
        P("req", "head", "seq"),
        P("req", "head", "seq", None),
        P("req", "head", "seq"),
        P("head", "seq"),
        P("req"),
        P("req"),
        P("req", None),
    )
    return jax.shard_map(
        on_device, mesh=mesh, in_specs=placed, out_specs=P("head", "req", "seq"), check_vma=False
    )
```
